512 devices in a mesh: lat: 16 (over z_lo, core), lon: 32 (over z_hi, x, y).
Axes of the slice: x: 4, y: 4, z: 16 (z_hi: 2, z_lo: 8; z = z_hi * 8 + z_lo), core: 2. Of those that a mesh axis runs over, the one named last changes fastest.
Arguments:
- fields: float32 [2, 2, 192, 192, 192], P(None, None, 'lat', 'lon'), may hold values from -60 to 60
- cotangent: float32 [2, 2, 192, 192, 192], P(None, None, 'lat', 'lon'), may hold values from -0.75 to 0.75
- keep_mask: int32 [2, 2], replicated, may hold values from 0 to 1, as said below
- region_ids: int32 [2, 192, 192], P(None, 'lat', 'lon'), may hold values from 0 to 2
- norm1_gain: float32 [192], replicated, may hold values from 0.25 to 1.75
- norm1_shift: float32 [192], replicated, may hold values from -3 to 3
- qkv_weight: float32 [192, 576], replicated, may hold values from -0.4375 to 0.4375
- qkv_bias: float32 [576], replicated, may hold values from -3 to 3
- position_table: float32 [16, 6, 6336], P('lat'), may hold values from -4 to 410
- proj_weight: float32 [192, 192], replicated, may hold values from -0.4375 to 0.4375
- proj_bias: float32 [192], replicated, may hold values from -3 to 3
- norm2_gain: float32 [192], replicated, may hold values from 0.25 to 1.75
- norm2_shift: float32 [192], replicated, may hold values from -3 to 3
- mlp_in_weight: float32 [192, 768], replicated, may hold values from -0.4375 to 0.4375
- mlp_in_bias: float32 [768], replicated, may hold values from -3 to 3
- mlp_out_weight: float32 [768, 192], replicated, may hold values from -0.21875 to 0.21875
Outputs:
- fields_grad: float32 [2, 2, 192, 192, 192], P(None, None, 'lat', 'lon')
- norm1_gain_grad: float32 [192], replicated
- norm1_shift_grad: float32 [192], replicated
- qkv_weight_grad: float32 [192, 576], P('lon')
- qkv_bias_grad: float32 [576], replicated
- table_grad: float32 [16, 6, 6336], P('lat')
- proj_weight_grad: float32 [192, 192], P('lon')
- proj_bias_grad: float32 [192], replicated
- norm2_gain_grad: float32 [192], replicated
- norm2_shift_grad: float32 [192], replicated
- mlp_in_weight_grad: float32 [192, 768], P('lon')
- mlp_in_bias_grad: float32 [768], replicated
- mlp_out_weight_grad: float32 [768, 192], P('lon')
The draws below stay inside these ranges and needn't reach their ends.
Inputs may be any that keep to these rules, and one draw needn't show every extreme that they name: `keep_mask`: each of the two columns holds at least one 1 and at least one 0.
All inputs are finite; a program needn't handle non-finite values.
Results may differ from the reference program's by a relative error of at most 0.00013.
Values sent between devices are 32-bit elements; how exact they have to be, the bound alone decides.
A program may use at most 128 MiB of HBM per device.

```python
import math
import jax
import jax.numpy as jnp
from jax import lax

C = 192
HEADS = 6
MLP = 768
WZ = 2
WH = 12
WW = 6
BATCH = 2
NTOK = 144
NH = 192
NW = 192
TYPES = 16
N_LON = 32


def draw_fields(key, part):
    key = jax.random.fold_in(key, 11)
    subkeys = jax.random.split(key, 3)
    full_shape = (BATCH, WZ, NH, NW, C)
    channel_scale = jnp.exp(jax.random.uniform(subkeys[1], (C,), jnp.float32, 0.0, math.log(10.0)))
    token_scale = jnp.exp(jax.random.uniform(subkeys[2], (BATCH, WZ, NH, NW, 1), jnp.float32, 0.0, math.log(10.0)))
    noise_base = jax.random.normal(subkeys[0], full_shape, jnp.float32)
    return jnp.clip(noise_base * channel_scale * token_scale * 0.1, -60.0, 60.0)


def draw_keep_mask(key, part):
    key = jax.random.fold_in(key, 37)
    subkeys = jax.random.split(key, 3)
    base_flags = (jax.random.randint(subkeys[0], (BATCH, 2), 0, 5) > 0).astype(jnp.int32)
    ones_row = jax.random.randint(subkeys[1], (2,), 0, BATCH)
    step_row = jax.random.randint(subkeys[2], (2,), 1, BATCH)
    zeros_row = (ones_row + step_row) % BATCH
    sample_rows = jnp.arange(BATCH)[:, None]
    flags = jnp.where(sample_rows == ones_row[None, :], 1, base_flags)
    flags = jnp.where(sample_rows == zeros_row[None, :], 0, flags)
    return flags.astype(jnp.int32)


def draw_position_table(key, part):
    key = jax.random.fold_in(key, 23)
    subkeys = jax.random.split(key, 1)
    relative = 2 * WW - 1
    full_shape = (NH // WH, HEADS, WZ, WZ, WH, WH, relative)
    table_out = jnp.clip(jax.random.normal(subkeys[0], full_shape, jnp.float32), -4.0, 4.0)
    return table_out.reshape(NH // WH, HEADS, WZ * WZ * WH * WH * relative)


def set_ends(drawn, stream_key, least, largest):
    index_at = [jax.random.randint(jax.random.fold_in(stream_key, axis), (), 0, length) for axis, length in enumerate(drawn.shape)]
    main_axis = drawn.shape.index(max(drawn.shape))
    neighbour = index_at[:main_axis] + [(index_at[main_axis] + 1) % drawn.shape[main_axis]] + index_at[main_axis + 1:]
    return drawn.at[tuple(index_at)].set(least).at[tuple(neighbour)].set(largest)


def block_scale(rng, shape, pieces, smallest, top_value):
    gain, own = 1.0, jax.random.fold_in(rng, 6)
    for dim, blocks in pieces:
        steps = jnp.exp(jax.random.uniform(jax.random.fold_in(own, dim), (blocks,), jnp.float32, smallest / len(pieces), top_value / len(pieces)))
        gain = gain * jnp.repeat(steps, shape[dim] // blocks).reshape([-1 if axis == dim else 1 for axis in range(len(shape))])
    return gain


def centred(key, extent, width, limit, shards=(), kind=jnp.bfloat16):
    values = width * jax.random.normal(key, extent, jnp.float32)
    if shards:
        values = values * block_scale(key, extent, shards, -0.22, 0.18)
    return jnp.clip(values, -limit, limit).astype(kind)


def setup_inputs(seed: int = 0) -> dict:
    key_of = jax.random.split(jax.random.key(seed), 17)
    fields = draw_fields(jax.random.fold_in(key_of[16], 71), 0)
    cotangent = centred(key_of[1], (BATCH, WZ, NH, NW, C), 0.05, 0.75, ((2, 16), (3, 32)), jnp.float32)
    keep_mask = draw_keep_mask(jax.random.fold_in(key_of[16], 71), 0)
    region_ids = set_ends(jax.random.randint(key_of[3], (WZ, NH, NW), 0, 3), jax.random.fold_in(key_of[3], 1), 0, 2).astype(jnp.int32)
    norm1_gain = jnp.clip(1.0 + 0.15 * jax.random.normal(key_of[4], (C,), jnp.float32), 0.25, 1.75)
    norm1_shift = centred(key_of[5], (C,), 0.5, 3.0, (), jnp.float32)
    qkv_weight = centred(key_of[6], (C, 3 * C), C ** -0.5, 0.4375, (), jnp.float32)
    qkv_bias = centred(key_of[7], (3 * C,), 0.5, 3.0, (), jnp.float32)
    position_table = draw_position_table(jax.random.fold_in(key_of[16], 71), 0)
    proj_weight = centred(key_of[9], (C, C), C ** -0.5, 0.4375, (), jnp.float32)
    proj_bias = centred(key_of[10], (C,), 0.5, 3.0, (), jnp.float32)
    norm2_gain = jnp.clip(1.0 + 0.15 * jax.random.normal(key_of[11], (C,), jnp.float32), 0.25, 1.75)
    norm2_shift = centred(key_of[12], (C,), 0.5, 3.0, (), jnp.float32)
    mlp_in_weight = centred(key_of[13], (C, MLP), C ** -0.5, 0.4375, (), jnp.float32)
    mlp_in_bias = centred(key_of[14], (MLP,), 0.5, 3.0, (), jnp.float32)
    mlp_out_weight = centred(key_of[15], (MLP, C), MLP ** -0.5, 0.21875, (), jnp.float32)
    return {"fields": fields, "cotangent": cotangent, "keep_mask": keep_mask, "region_ids": region_ids, "norm1_gain": norm1_gain, "norm1_shift": norm1_shift, "qkv_weight": qkv_weight, "qkv_bias": qkv_bias, "position_table": position_table, "proj_weight": proj_weight, "proj_bias": proj_bias, "norm2_gain": norm2_gain, "norm2_shift": norm2_shift, "mlp_in_weight": mlp_in_weight, "mlp_in_bias": mlp_in_bias, "mlp_out_weight": mlp_out_weight}


keep_rate = 0.8
norm_eps = 1e-05
top_precision = lax.Precision.HIGHEST

def layer_norm(values, norm_gain, norm_shift):
    center = values - lax.optimization_barrier(jnp.mean(values, axis=-1, keepdims=True))
    spread = lax.optimization_barrier(jnp.mean(center * center, axis=-1, keepdims=True))
    return center * lax.rsqrt(spread + norm_eps) * norm_gain + norm_shift

def position_bias(table_rows, levels_win, lat_rows, lon_cols):
    leading = table_rows.shape[:-1]
    relative = 2 * lon_cols - 1
    token_count = levels_win * lat_rows * lon_cols
    token_ids = jnp.arange(token_count, dtype=jnp.int32)
    level_of = token_ids // (lat_rows * lon_cols)
    row_of = token_ids // lon_cols % lat_rows
    col_of = token_ids % lon_cols
    position = (level_of[:, None] * levels_win + level_of[None, :]) * lat_rows + row_of[:, None]
    position = (position * lat_rows + row_of[None, :]) * relative + col_of[:, None] - col_of[None, :] + lon_cols - 1
    picked = jnp.take(table_rows, position.reshape(-1).astype(jnp.int32), axis=-1)
    return picked.reshape(leading + (token_count, token_count))

def attend(windows, qkv_weight, qkv_bias, table_rows, proj_weight, proj_bias, regions, levels_win, lat_rows, lon_cols):
    leading = windows.shape[:-2]
    token_count = windows.shape[-2]
    features = windows.shape[-1]
    head_count = table_rows.shape[-2]
    head_width = features // head_count
    projected = jnp.matmul(windows, qkv_weight, precision=top_precision) + qkv_bias
    projected = projected.reshape(leading + (token_count, 3, head_count, head_width))
    query_matrix = projected[..., 0, :, :]
    key_matrix = projected[..., 1, :, :]
    value_matrix = projected[..., 2, :, :]
    logit_scores = jnp.einsum('...zjx,...pjx->...jzp', query_matrix, key_matrix, precision=top_precision) / math.sqrt(head_width)
    logit_scores = logit_scores + position_bias(table_rows, levels_win, lat_rows, lon_cols)
    same_region = regions[..., :, None] == regions[..., None, :]
    logit_scores = jnp.where(same_region[..., None, :, :], logit_scores, -1e+30)
    softmax_weights = jax.nn.softmax(logit_scores, axis=-1)
    merged_head_output = jnp.einsum('...kwa,...aks->...wks', softmax_weights, value_matrix, precision=top_precision)
    merged_head_output = merged_head_output.reshape(leading + (token_count, features))
    return jnp.matmul(merged_head_output, proj_weight, precision=top_precision) + proj_bias

def mlp_branch(values, norm_gain, norm_shift, in_weight, in_bias, out_weight):
    normed = layer_norm(values, norm_gain, norm_shift)
    hidden = jax.nn.gelu(jnp.matmul(normed, in_weight, precision=top_precision) + in_bias, approximate=False)
    return jnp.matmul(hidden, out_weight, precision=top_precision)

def sample_forward(sample, keep_row, region_ids, params):
    norm1_gain, norm1_shift, qkv_weight, qkv_bias, position_table, proj_weight, proj_bias, norm2_gain, norm2_shift, mlp_in_weight, mlp_in_bias, mlp_out_weight = params
    keep_factor = keep_row.astype(jnp.float32) / keep_rate
    normed = layer_norm(sample, norm1_gain, norm1_shift)
    shifted = jnp.roll(normed, (-(WZ // 2), -(WH // 2), -(WW // 2)), axis=(0, 1, 2))
    windows = shifted.reshape(WZ, TYPES, WH, N_LON, WW, C).transpose(1, 3, 0, 2, 4, 5).reshape(TYPES, N_LON, NTOK, C)
    regions = region_ids.reshape(WZ, TYPES, WH, N_LON, WW).transpose(1, 3, 0, 2, 4).reshape(TYPES, N_LON, NTOK)
    branch = attend(windows, qkv_weight, qkv_bias, position_table[:, None], proj_weight, proj_bias, regions, WZ, WH, WW)
    branch = branch.reshape(TYPES, N_LON, WZ, WH, WW, C).transpose(2, 0, 3, 1, 4, 5).reshape(WZ, NH, NW, C)
    branch = jnp.roll(branch, (WZ // 2, WH // 2, WW // 2), axis=(0, 1, 2))
    middle = sample + keep_factor[0] * branch
    feed = mlp_branch(middle, norm2_gain, norm2_shift, mlp_in_weight, mlp_in_bias, mlp_out_weight)
    return middle + keep_factor[1] * feed

def reference(fields, cotangent, keep_mask, region_ids, norm1_gain, norm1_shift, qkv_weight, qkv_bias, position_table, proj_weight, proj_bias, norm2_gain, norm2_shift, mlp_in_weight, mlp_in_bias, mlp_out_weight):
    params = (norm1_gain, norm1_shift, qkv_weight, qkv_bias, position_table, proj_weight, proj_bias, norm2_gain, norm2_shift, mlp_in_weight, mlp_in_bias, mlp_out_weight)

    def one_sample(sample_items):
        sample, sample_cot, keep_row = sample_items

        def forward(values, weights):
            return sample_forward(values, keep_row, region_ids, weights)
        backward = jax.vjp(forward, sample, params)[1]
        return backward(sample_cot)
    sample_grads, param_grads = lax.map(one_sample, (fields, cotangent, keep_mask))
    summed = jax.tree.map(lambda grad_part: lax.optimization_barrier(jnp.sum(grad_part, axis=0)), param_grads)
    return (sample_grads, summed[0], summed[1], summed[2], summed[3], summed[4], summed[5], summed[6], summed[7], summed[8], summed[9], summed[10], summed[11])
```

```python
import functools
import math

import jax
import jax.numpy as jnp
import numpy as np
from jax import lax
from jax.experimental import pallas as pl
from jax.experimental.pallas import tpu as pltpu
from jax.sharding import PartitionSpec as P

f32 = jnp.float32
bf16 = jnp.bfloat16
MESH = pl.DeviceIdType.MESH
C = 192
HEADS = 6
HID = 768
TOK = 144
ZH = 24
REL = 11
FLAT = 132
eps = 1e-05
kept = 1.25
scale = 1.0 / math.sqrt(32.0)
VMEM_LIMIT = 56 * 1024 * 1024


def bias_order():
    to = np.zeros((384, 384), np.float32)
    rest = np.zeros((384, 128), np.float32)
    for z in range(2):
        for h in range(12):
            for r in range(REL):
                lane = z * FLAT + h * REL + r
                spot = (REL - 1 - r) * ZH + (h // 6) * 12 + z * 6 + h % 6
                to[lane, spot] = 1.0
                if lane >= 256:
                    for head in range(HEADS):
                        rest[spot, 8 * head + lane - 256] = 1.0
    return to, rest


def spread_order():
    to = np.zeros((C, 256), np.float32)
    for feature in range(C):
        to[feature, 8 * (feature // 6) + feature % 6] = 1.0
    return to


def halves(values):
    high = values.astype(bf16)
    return high, (values - high.astype(f32)).astype(bf16)


def thirds(values):
    high = values.astype(bf16)
    left = values - high.astype(f32)
    mid = left.astype(bf16)
    return high, mid, (left - mid.astype(f32)).astype(bf16)


def one(a, b, ca, cb):
    return lax.dot_general(a, b, (((ca,), (cb,)), ((), ())), preferred_element_type=f32)


def product(a, b, ca=1, cb=0):
    return one(a[0], b[0], ca, cb) + (one(a[0], b[1], ca, cb) + one(a[1], b[0], ca, cb))


def norm_parts(values):
    center = values - jnp.mean(values, axis=-1, keepdims=True)
    spread = jnp.mean(center * center, axis=-1, keepdims=True)
    inv = lax.rsqrt(spread + eps)
    return center * inv, inv


def norm_back(grad, gain, unit, inv):
    scaled = grad * gain
    return inv * (
        scaled
        - jnp.mean(scaled, axis=-1, keepdims=True)
        - unit * jnp.mean(scaled * unit, axis=-1, keepdims=True)
    )


def token_row(hh, wh, w3):
    return (wh * 3 + w3) * ZH + hh * 12


def neighbour(lat, lon, lats, lons, dlat, dlon):
    return lax.rem(lat + dlat + lats, lats), lax.rem(lon + dlon + lons, lons)


def halo_kernel(lats, lons, keep, fields, cot, win, loc, out_buf, in_buf, send_sem, recv_sem):
    lat = lax.axis_index("lat")
    lon = lax.axis_index("lon")
    at = functools.partial(neighbour, lat, lon, lats, lons)
    barrier = pltpu.get_barrier_semaphore()
    for dlat, dlon in ((1, 0), (0, 1), (1, 1)):
        pl.semaphore_signal(barrier, inc=1, device_id=at(dlat, dlon), device_id_type=MESH)
    attn = 1 - keep[0, 0]

    def rows(sample, sh, sw, w3, zz):
        part = (sample, 1 - zz, pl.ds(sh * 6, 6), sw * 3 + w3, slice(None))
        return jnp.concatenate([fields[part], cot[part]], axis=-1)

    copies = []
    for slot, (sh, sw) in enumerate(((0, 0), (0, 1), (1, 0))):
        for w3 in range(3):
            for zz in range(2):
                out_buf[slot, pl.ds(w3 * 12 + zz * 6, 6), :] = rows(attn, sh, sw, w3, zz)
        if slot == 0:
            pl.semaphore_wait(barrier, 3)
        copy = pltpu.make_async_remote_copy(
            src_ref=out_buf.at[slot],
            dst_ref=in_buf.at[slot],
            send_sem=send_sem.at[slot],
            recv_sem=recv_sem.at[slot],
            device_id=at(-1 if sh == 0 else 0, -1 if sw == 0 else 0),
            device_id_type=MESH,
        )
        copy.start()
        copies.append(copy)
    for w3 in range(3):
        for zz in range(2):
            win[pl.ds(token_row(0, 0, w3) + zz * 6, 6), :] = rows(attn, 1, 1, w3, zz)
            for sh in range(2):
                for sw in range(2):
                    start = token_row(1 - sh, 1 - sw, w3) + zz * 6
                    loc[pl.ds(start, 6), :] = rows(1 - attn, sh, sw, w3, zz)
    for slot, (sh, sw) in enumerate(((0, 0), (0, 1), (1, 0))):
        copies[slot].wait_recv()
        for w3 in range(3):
            start = token_row(1 - sh, 1 - sw, w3)
            win[pl.ds(start, 12), :] = in_buf[slot, pl.ds(w3 * 12, 12), :]
    for copy in copies:
        copy.wait_send()


def compute_kernel(
    keep, win, loc, region, n1g, n1s, wqkv, bqkv, table, wproj, bproj, n2g, n2s, win_w, b_in, wout,
    order, rest, spread,
    large, tabs, dxa, other,
    tab_in, bias_s, attn_s, diff_s, qp_s, mi_s, mo_s, row_s, tab_s,
):
    x = win[:, 0:C]
    cot = win[:, C : 2 * C]
    unit1, inv1 = norm_parts(x)
    gain1 = n1g[...].reshape(1, C)
    normed1 = halves(unit1 * gain1 + n1s[...].reshape(1, C))
    w_qkv = halves(wqkv[...])
    proj = product(normed1, w_qkv) + bqkv[...].reshape(1, 3 * C)
    query = halves(proj[:, 0:C] * scale)
    key = halves(proj[:, C : 2 * C])
    value = halves(proj[:, 2 * C : 3 * C])

    tab_in[...] = jnp.zeros(tab_in.shape, f32)
    for zn in range(2):
        for hn in range(12):
            spot = (hn // 6) * 12 + zn * 6 + hn % 6
            for zm in range(2):
                start = ((zn * 2 + zm) * 12 + hn) * FLAT
                tab_in[pl.ds(spot * 8, HEADS), zm * FLAT : (zm + 1) * FLAT] = table[0, :, start : start + FLAT]
    shifted = None
    for part in thirds(tab_in[...]):
        term = one(part, order[...], 1, 0)
        shifted = term if shifted is None else shifted + term
    for l in range(3):
        bias_s[l] = shifted[:, l * 128 : l * 128 + 128]

    marks = region[...].astype(f32)
    columns = []
    for w in range(6):
        for hh in range(2):
            for z in range(2):
                columns.append(jnp.broadcast_to(marks[z, hh * 6 : hh * 6 + 6, w : w + 1], (6, TOK)))
    mark_rows = jnp.concatenate(columns, axis=0)
    same = mark_rows == mark_rows.T

    lanes = lax.broadcasted_iota(jnp.int32, (1, C), 1)
    masks = [(lanes // 32 == h) for h in range(HEADS)]

    def masked(pair, h):
        zero = jnp.zeros((), bf16)
        return tuple(jnp.where(masks[h], part, zero) for part in pair)

    mixed = jnp.zeros((TOK, C), f32)
    for h in range(HEADS):
        scores = product(masked(query, h), key, 1, 1)
        strip = jnp.concatenate([bias_s[l, pl.ds(h, ZH, stride=8), :] for l in range(3)], axis=1)
        bias = jnp.concatenate(
            [pltpu.roll(strip, (384 - (5 - wn) * ZH) % 384, axis=1)[:, 0:TOK] for wn in range(6)], axis=0
        )
        scores = jnp.where(same, scores + bias, -1e30)
        scores = jnp.exp(scores - jnp.max(scores, axis=-1, keepdims=True))
        attn = scores / jnp.sum(scores, axis=-1, keepdims=True)
        attn_s[h] = attn
        mixed = mixed + product(halves(attn), masked(value, h))
    mixed = halves(mixed)
    w_proj = halves(wproj[...])
    branch = product(mixed, w_proj) + bproj[...].reshape(1, C)

    both = keep[0, 0] == keep[0, 1]
    loc_x = loc[:, 0:C]
    loc_cot = loc[:, C : 2 * C]
    middle = jnp.where(both, x + kept * branch, loc_x)
    cot_m = jnp.where(both, cot, loc_cot)
    unit2, inv2 = norm_parts(middle)
    gain2 = n2g[...].reshape(1, C)
    normed2 = halves(unit2 * gain2 + n2s[...].reshape(1, C))
    w_in = halves(win_w[...])
    hidden = product(normed2, w_in) + b_in[...].reshape(1, HID)
    cdf = 0.5 * (1.0 + lax.erf(hidden * math.sqrt(0.5)))
    slope = cdf + hidden * jnp.exp(-0.5 * hidden * hidden) * (1.0 / math.sqrt(2.0 * math.pi))
    grad_y = halves(kept * cot_m)
    w_out = halves(wout[...])
    grad_hidden = halves(product(grad_y, w_out, 1, 1) * slope)
    mo_s[:, 0:C] = product(halves(hidden * cdf), grad_y, 0, 0)

    ones_lane = (lax.broadcasted_iota(jnp.int32, (1, 256), 1) & 7) == 6

    def spread_out(pair):
        high = one(pair[0], spread[...], 1, 0)
        low = one(pair[1], spread[...], 1, 0)
        return jnp.where(ones_lane, 1.0, high).astype(bf16), low.astype(bf16)

    mi_s[...] = product(spread_out(normed2), grad_hidden, 0, 0)
    grad_n2 = product(grad_hidden, w_in, 1, 1)
    row_s[0:1, 2 * C : 3 * C] = jnp.sum(grad_n2 * unit2, axis=0, keepdims=True)
    row_s[0:1, 3 * C : 4 * C] = jnp.sum(grad_n2, axis=0, keepdims=True)
    grad_m = cot_m + norm_back(grad_n2, gain2, unit2, inv2)
    grad_a = jnp.where(both, grad_m, cot)
    other[...] = jnp.where(both, loc_cot, grad_m)

    grad_b = halves(kept * grad_a)
    qp_s[:, 3 * C : 4 * C] = product(spread_out(mixed), grad_b, 0, 0)
    grad_o = halves(product(grad_b, w_proj, 1, 1))
    grad_q = jnp.zeros((TOK, C), f32)
    grad_k = jnp.zeros((TOK, C), f32)
    grad_v = jnp.zeros((TOK, C), f32)
    diff_s[...] = jnp.zeros(diff_s.shape, f32)
    for h in range(HEADS):
        attn = attn_s[h]
        grad_oh = masked(grad_o, h)
        grad_attn = product(grad_oh, value, 1, 1)
        grad_v = grad_v + product(halves(attn), grad_oh, 0, 0)
        term = attn * grad_attn
        grad_s = term - attn * jnp.sum(term, axis=-1, keepdims=True)
        grad_sp = halves(grad_s)
        grad_q = grad_q + product(grad_sp, masked(key, h))
        grad_k = grad_k + product(grad_sp, masked(query, h), 0, 0)
        wide = jnp.concatenate([grad_s, jnp.zeros((TOK, 384 - TOK), f32)], axis=1)
        total = None
        for wn in range(6):
            block = wide[wn * ZH : (wn + 1) * ZH, :]
            if wn < 5:
                block = pltpu.roll(block, (5 - wn) * ZH, axis=1)
            total = block if total is None else total + block
        for l in range(3):
            diff_s[l, pl.ds(h, ZH, stride=8), :] = total[:, l * 128 : l * 128 + 128]
    grad_p = halves(jnp.concatenate([grad_q * scale, grad_k, grad_v], axis=1))
    qp_s[:, 0 : 3 * C] = product(spread_out(normed1), grad_p, 0, 0)
    grad_n1 = product(grad_p, w_qkv, 1, 1)
    row_s[0:1, 0:C] = jnp.sum(grad_n1 * unit1, axis=0, keepdims=True)
    row_s[0:1, C : 2 * C] = jnp.sum(grad_n1, axis=0, keepdims=True)
    grad_x = grad_a + norm_back(grad_n1, gain1, unit1, inv1)
    for hh in range(2):
        for wh in range(2):
            for w3 in range(3):
                start = token_row(hh, wh, w3)
                dxa[hh * 2 + wh, pl.ds(w3 * 12, 12), :] = grad_x[start : start + 12, :]

    diff = halves(jnp.concatenate([diff_s[l] for l in range(3)], axis=1))
    back = one(diff[0], order[...], 1, 1) + one(diff[1], order[...], 1, 1)
    tail = one(diff[0], rest[...], 1, 0) + one(diff[1], rest[...], 1, 0)
    row_id = lax.broadcasted_iota(jnp.int32, tail.shape, 0) & 7
    lane_id = lax.broadcasted_iota(jnp.int32, tail.shape, 1) // 8
    tail = jnp.where(row_id == lane_id, tail, 0.0).reshape(ZH, 8, 128).sum(axis=1)
    for l in range(2):
        tab_s[l] = back[:, l * 128 : l * 128 + 128]
    tab_s[0, pl.ds(6, ZH, stride=8), :] = tail
    for k in range(8):
        for l in range(2):
            tabs[2 * k + l] = tab_s[l, 24 * k : 24 * k + 24, :]

    mi_rows = lax.broadcasted_iota(jnp.int32, (256, 1), 0) & 7
    mi_s[...] = jnp.where(mi_rows == 7, row_s[0:1, :], mi_s[...])
    low_lanes = lax.broadcasted_iota(jnp.int32, (8, 128), 1) < 64

    def pack(j, carry):
        a = lax.rem(j // 4, 4)
        b = lax.rem(j, 4)
        zh = j // 16
        at8 = pl.ds(pl.multiple_of(j * 8, 8), 8)

        def put(piece, tile, rows=slice(None)):
            if piece < 8:
                large[0, a, b, zh, piece, rows, :] = tile
            else:
                large[1, b, a, zh, piece - 8, rows, :] = tile

        for piece in range(6):
            put(piece, qp_s[at8, piece * 128 : piece * 128 + 128])
            put(piece + 6, mi_s[at8, piece * 128 : piece * 128 + 128])
        tails = []
        for k in range(3):
            at = pl.ds(pl.multiple_of(j * 24 + k * 8, 8), 8)
            put(12 + k, mo_s[at, 0:128])
            tails.append(mo_s[at, 128:256])
        put(15, jnp.where(low_lanes, tails[0], pltpu.roll(tails[1], 64, axis=1)))
        pairs = jnp.where(low_lanes, tails[2], pltpu.roll(pltpu.roll(tails[2], 64, axis=1), 7, axis=0))
        for k in range(4):
            put(k, pairs[2 * k : 2 * k + 1, :], slice(7, 8))
        return carry

    lax.fori_loop(0, 32, pack, 0)


def sums_kernel(
    lats, lons, keep, large, tabs, dxa, other,
    fields_grad, n1g_o, n1s_o, qkvw_o, qkvb_o, table_o, projw_o, projb_o, n2g_o, n2s_o, inw_o, inb_o, outw_o,
    back_in, pair_in, a_in, b_in, z_in, gather, tab_in, tab_pair, tab_sum, tab_all, acc_a, acc_b, mine, wide_s,
    back_ss, back_rs, pair_ss, pair_rs, a_ss, a_rs, b_ss, b_rs, z_ss, z_rs, g_ss, g_rs, t_ss, t_rs, tp_ss, tp_rs, tg_ss, tg_rs,
):
    lat = lax.axis_index("lat")
    lon = lax.axis_index("lon")
    core = lax.rem(lat, 2)
    zl = lat // 2
    zh = lon // 16
    plane = lax.rem(lon, 16)
    px = plane // 4
    py = lax.rem(plane, 4)
    at = functools.partial(neighbour, lat, lon, lats, lons)

    barrier = pltpu.get_barrier_semaphore()

    def hello(device):
        pl.semaphore_signal(barrier, inc=1, device_id=device, device_id_type=MESH)

    for dlat, dlon in ((-1, 0), (0, -1), (-1, -1)):
        hello(at(dlat, dlon))
    for d in range(1, 16):
        hello((lax.rem(lat + d, 16), lon))
        hello((lat, zh * 16 + lax.rem(plane + d, 16)))
    for d in range(8):
        hello((lax.rem(lat + 2 * d, 16), lax.rem(lon + 16, 32)))
    pl.semaphore_wait(barrier, 3 + 30 + 8)

    def send(src, dst, ss, rs, device):
        copy = pltpu.make_async_remote_copy(
            src_ref=src, dst_ref=dst, send_sem=ss, recv_sem=rs, device_id=device, device_id_type=MESH
        )
        copy.start()
        return copy

    every = []

    pair = send(large.at[1 - core], pair_in, pair_ss, pair_rs, (lat + 1 - 2 * core, lon))
    every.append(pair)
    home = []
    for slot, (hh, wh) in enumerate(((1, 1), (1, 0), (0, 1))):
        home.append(send(dxa.at[hh * 2 + wh], back_in.at[slot], back_ss.at[slot], back_rs.at[slot], at(hh, wh)))
    every += home
    tab_copies = []
    for d in range(1, 16):
        to = lax.rem(plane + d, 16)
        tab_copies.append(
            send(tabs.at[to], tab_in.at[d - 1], t_ss.at[d - 1], t_rs.at[d - 1], (lat, zh * 16 + to))
        )
    every += tab_copies

    pair.wait_recv()

    def add_pair(i, carry):
        for j in range(4):
            pair_in[i, j] = pair_in[i, j] + large[core, i, j]
        return carry

    lax.fori_loop(0, 4, add_pair, 0)
    first = px + core * (py - px)
    second = py + core * (px - py)

    def along(pos_first, pos_second):
        x = pos_first + core * (pos_second - pos_first)
        y = pos_second + core * (pos_first - pos_second)
        return lat, zh * 16 + x * 4 + y

    a_copies = []
    for d in range(1, 4):
        to = lax.rem(first + d, 4)
        a_copies.append(
            send(pair_in.at[to], a_in.at[d - 1], a_ss.at[d - 1], a_rs.at[d - 1], along(to, second))
        )
    every += a_copies

    for copy in tab_copies:
        copy.wait_recv()
    total = tabs[plane]
    for d in range(15):
        total = total + tab_in[d]
    tab_sum[...] = total
    tab_across = send(tab_sum, tab_pair, tp_ss, tp_rs, (lat, lax.rem(lon + 16, 32)))
    every.append(tab_across)

    for copy in a_copies:
        copy.wait_recv()
    for j in range(4):
        acc_a[j] = (pair_in[first, j] + a_in[0, j]) + (a_in[1, j] + a_in[2, j])
    b_copies = []
    for d in range(1, 4):
        to = lax.rem(second + d, 4)
        b_copies.append(send(acc_a.at[to], b_in.at[d - 1], b_ss.at[d - 1], b_rs.at[d - 1], along(first, to)))
    every += b_copies

    tab_across.wait_recv()
    tab_all[plane] = tab_sum[...] + tab_pair[...]
    tab_back = []
    for d in range(1, 16):
        to = lax.rem(plane + d, 16)
        tab_back.append(
            send(tab_all.at[plane], tab_all.at[plane], tg_ss.at[d - 1], tg_rs.at[d - 1], (lat, zh * 16 + to))
        )
    every += tab_back

    for copy in b_copies:
        copy.wait_recv()
    acc_b[...] = (acc_a[second] + b_in[0]) + (b_in[1] + b_in[2])
    z_copies = []
    for d in range(1, 16):
        to = lax.rem(zh * 8 + zl + d, 16)
        z_copies.append(
            send(
                acc_b.at[to // 8, lax.rem(to, 8)], z_in.at[d - 1], z_ss.at[d - 1], z_rs.at[d - 1],
                (lax.rem(to, 8) * 2 + core, (to // 8) * 16 + plane),
            )
        )
    every += z_copies

    for copy in home:
        copy.wait_recv()
    first_kept = keep[0, 0] == 1
    for sh in range(2):
        for sw in range(2):
            for w3 in range(3):
                if (sh, sw) == (1, 1):
                    from_a = dxa[0, pl.ds(w3 * 12, 12), :]
                else:
                    from_a = back_in[sh * 2 + sw, pl.ds(w3 * 12, 12), :]
                from_o = other[pl.ds(token_row(1 - sh, 1 - sw, w3), 12), :]
                tops = (jnp.where(first_kept, from_a, from_o), jnp.where(first_kept, from_o, from_a))
                for sample in range(2):
                    for zz in range(2):
                        fields_grad[sample, 1 - zz, pl.ds(sh * 6, 6), sw * 3 + w3, :] = tops[sample][
                            zz * 6 : zz * 6 + 6, :
                        ]

    for copy in z_copies:
        copy.wait_recv()
    total = acc_b[zh, zl]
    for d in range(15):
        total = total + z_in[d]
    slot = core * 8 + zl
    gather[slot] = total
    mine[...] = total
    g_copies = []
    for d in range(1, 16):
        to = lax.rem(lat + d, 16)
        g_copies.append(send(mine, gather.at[slot], g_ss.at[d - 1], g_rs.at[d - 1], (to, lon)))
    every += g_copies

    for copy in tab_back:
        copy.wait_recv()
    for k in range(8):
        for l in range(2):
            wide_s[l, 24 * k : 24 * k + 24, :] = tab_all[2 * k + l]
    tail = wide_s[0, pl.ds(6, ZH, stride=8), :]
    for h in range(HEADS):
        moved = tail if h == 0 else pltpu.roll(tail, 128 - 8 * h, axis=1)
        wide_s[2, pl.ds(h, ZH, stride=8), :] = moved
    for zn in range(2):
        for hn in range(12):
            spot = (hn // 6) * 12 + zn * 6 + hn % 6
            block = jnp.concatenate([wide_s[l, spot * 8 : spot * 8 + 8, :] for l in range(3)], axis=1)
            for zm in range(2):
                start = ((zn * 2 + zm) * 12 + hn) * FLAT
                table_o[0, :, start : start + FLAT] = block[0:HEADS, zm * FLAT : (zm + 1) * FLAT]

    for copy in g_copies:
        copy.wait_recv()

    def strip(first_piece, count, row, rows):
        return jnp.concatenate([gather[p, row : row + rows, :] for p in range(first_piece, first_piece + count)], axis=1)

    sums = strip(0, 6, 0, 6)
    qkvw_o[...] = sums[:, 0 : 3 * C]
    projw_o[...] = sums[:, 3 * C : 4 * C]
    inw_o[...] = strip(6, 6, 0, 6)
    small = strip(0, 6, 6, 1)
    qkvb_o[...] = small[:, 0 : 3 * C].reshape(3 * C)
    projb_o[...] = small[:, 3 * C : 4 * C].reshape(C)
    inb_o[...] = strip(6, 6, 6, 1).reshape(HID)
    norms = strip(6, 6, 7, 1)
    for i, ref in enumerate((n1g_o, n1s_o, n2g_o, n2s_o)):
        ref[...] = norms[:, i * C : (i + 1) * C].reshape(C)
    for k in range(3):
        outw_o[8 * k : 8 * k + 8, 0:128] = gather[12 + k]
    outw_o[0:8, 128:192] = gather[15, :, 0:64]
    outw_o[8:16, 128:192] = pltpu.roll(gather[15], 64, axis=1)[:, 0:64]
    for k in range(4):
        line = gather[k, 7:8, :]
        outw_o[16 + 2 * k : 17 + 2 * k, 128:192] = line[:, 0:64]
        outw_o[17 + 2 * k : 18 + 2 * k, 128:192] = pltpu.roll(line, 64, axis=1)[:, 0:64]
    for copy in every:
        copy.wait_send()


def shape(*dims):
    return jax.ShapeDtypeStruct(dims, f32)


def vmem():
    return pl.BlockSpec(memory_space=pltpu.VMEM)


def smem():
    return pl.BlockSpec(memory_space=pltpu.SMEM)


def per_device(lats, lons, fields, cotangent, keep_mask, region_ids, *weights):
    order, rest = (jnp.asarray(m, bf16) for m in bias_order())
    spread = jnp.asarray(spread_order(), bf16)
    dma = pltpu.SemaphoreType.DMA
    win, loc = pl.pallas_call(
        functools.partial(halo_kernel, lats, lons),
        out_shape=(shape(TOK, 2 * C), shape(TOK, 2 * C)),
        in_specs=[smem(), vmem(), vmem()],
        out_specs=(vmem(), vmem()),
        scratch_shapes=[
            pltpu.VMEM((3, 36, 2 * C), f32),
            pltpu.VMEM((3, 36, 2 * C), f32),
            dma((3,)),
            dma((3,)),
        ],
        compiler_params=pltpu.CompilerParams(collective_id=0, has_side_effects=True, vmem_limit_bytes=VMEM_LIMIT),
        name="halo_in",
    )(keep_mask, fields, cotangent)
    large, tabs, dxa, other = pl.pallas_call(
        compute_kernel,
        out_shape=(shape(2, 4, 4, 2, 8, 8, 128), shape(16, 24, 128), shape(4, 36, C), shape(TOK, C)),
        in_specs=[smem()] + [vmem()] * 18,
        out_specs=(vmem(),) * 4,
        scratch_shapes=[
            pltpu.VMEM((192, 384), f32),
            pltpu.VMEM((3, 192, 128), f32),
            pltpu.VMEM((HEADS, TOK, TOK), f32),
            pltpu.VMEM((3, 192, 128), f32),
            pltpu.VMEM((256, 768), f32),
            pltpu.VMEM((256, 768), f32),
            pltpu.VMEM((768, 256), f32),
            pltpu.VMEM((8, 768), f32),
            pltpu.VMEM((2, 192, 128), f32),
        ],
        compiler_params=pltpu.CompilerParams(vmem_limit_bytes=VMEM_LIMIT),
        name="block_both_ways",
    )(keep_mask, win, loc, region_ids, *weights, order, rest, spread)
    tile = (8, 128)
    return pl.pallas_call(
        functools.partial(sums_kernel, lats, lons),
        out_shape=(
            shape(2, 2, 12, 6, C), shape(C), shape(C), shape(6, 3 * C), shape(3 * C), shape(1, HEADS, 6336),
            shape(6, C), shape(C), shape(C), shape(C), shape(6, HID), shape(HID), shape(24, C),
        ),
        in_specs=[smem()] + [vmem()] * 4,
        out_specs=(vmem(),) * 13,
        scratch_shapes=[
            pltpu.VMEM((3, 36, C), f32),
            pltpu.VMEM((4, 4, 2, 8) + tile, f32),
            pltpu.VMEM((3, 4, 2, 8) + tile, f32),
            pltpu.VMEM((3, 2, 8) + tile, f32),
            pltpu.VMEM((15,) + tile, f32),
            pltpu.VMEM((16,) + tile, f32),
            pltpu.VMEM((15, 24, 128), f32),
            pltpu.VMEM((24, 128), f32),
            pltpu.VMEM((24, 128), f32),
            pltpu.VMEM((16, 24, 128), f32),
            pltpu.VMEM((4, 2, 8) + tile, f32),
            pltpu.VMEM((2, 8) + tile, f32),
            pltpu.VMEM(tile, f32),
            pltpu.VMEM((3, 192, 128), f32),
            dma((3,)), dma((3,)), dma, dma, dma((3,)), dma((3,)), dma((3,)), dma((3,)),
            dma((15,)), dma((15,)), dma((15,)), dma((15,)), dma((15,)), dma((15,)), dma, dma, dma((15,)), dma((15,)),
        ],
        compiler_params=pltpu.CompilerParams(collective_id=1, has_side_effects=True, vmem_limit_bytes=VMEM_LIMIT),
        name="gradient_sums",
    )(keep_mask, large, tabs, dxa, other)


def solution(mesh):
    grid = P(None, None, "lat", "lon", None)
    rows = P("lon", None)
    return jax.shard_map(
        functools.partial(per_device, mesh.shape["lat"], mesh.shape["lon"]),
        mesh=mesh,
        in_specs=(grid, grid, P(), P(None, "lat", "lon"), P(), P(), P(), P(), P("lat", None, None))
        + (P(),) * 7,
        out_specs=(grid, P(), P(), rows, P(), P("lat", None, None), rows, P(), P(), P(), rows, P(), rows),
        check_vma=False,
    )
```

```python
import functools
import math

import jax
import jax.numpy as jnp
import numpy as np
from jax import lax
from jax.experimental import pallas as pl
from jax.experimental.pallas import tpu as pltpu
from jax.sharding import PartitionSpec as P

f32 = jnp.float32
bf16 = jnp.bfloat16
MESH = pl.DeviceIdType.MESH
C = 192
HEADS = 6
HID = 768
TOK = 144
ZH = 24
REL = 11
FLAT = 132
eps = 1e-05
kept = 1.25
scale = 1.0 / math.sqrt(32.0)
VMEM_LIMIT = 56 * 1024 * 1024


def bias_order():
    to = np.zeros((384, 384), np.float32)
    rest = np.zeros((384, 128), np.float32)
    for z in range(2):
        for h in range(12):
            for r in range(REL):
                lane = z * FLAT + h * REL + r
                spot = (REL - 1 - r) * ZH + h * 2 + 1 - z
                to[lane, spot] = 1.0
                if lane >= 256:
                    for head in range(HEADS):
                        rest[spot, 8 * head + lane - 256] = 1.0
    return to, rest


def spread_order():
    to = np.zeros((C, 256), np.float32)
    for feature in range(C):
        to[feature, 8 * (feature // 6) + feature % 6] = 1.0
    return to


def halves(values):
    high = values.astype(bf16)
    return high, (values - high.astype(f32)).astype(bf16)


def thirds(values):
    high = values.astype(bf16)
    left = values - high.astype(f32)
    mid = left.astype(bf16)
    return high, mid, (left - mid.astype(f32)).astype(bf16)


def one(a, b, ca, cb):
    return lax.dot_general(a, b, (((ca,), (cb,)), ((), ())), preferred_element_type=f32)


def product(a, b, ca=1, cb=0):
    return one(a[0], b[0], ca, cb) + (one(a[0], b[1], ca, cb) + one(a[1], b[0], ca, cb))


def norm_parts(values):
    center = values - jnp.mean(values, axis=-1, keepdims=True)
    spread = jnp.mean(center * center, axis=-1, keepdims=True)
    inv = lax.rsqrt(spread + eps)
    return center * inv, inv


def norm_back(grad, gain, unit, inv):
    scaled = grad * gain
    return inv * (
        scaled
        - jnp.mean(scaled, axis=-1, keepdims=True)
        - unit * jnp.mean(scaled * unit, axis=-1, keepdims=True)
    )


def neighbour(lat, lon, lats, lons, dlat, dlon):
    return lax.rem(lat + dlat + lats, lats), lax.rem(lon + dlon + lons, lons)


def take_tokens(read):
    return jnp.concatenate([read(w).reshape(ZH, C) for w in range(6)], axis=0)


def put_tokens(write, values):
    for w in range(6):
        write(w, values[w * ZH : (w + 1) * ZH, :].reshape(12, 2, C))


def kernel_a(
    lats, lons,
    keep, fields, cotg, region, n1g, n1s, wqkv, bqkv, table, wproj, bproj, n2g, n2s, win_w, b_in, wout,
    order, rest, spread,
    gather, table_o, back, other,
    sel_x, sel_c, win_x, win_c, dxa,
    early, late, pair_e, pair_l, a_e, a_l, b_e, b_l, acc_ae, acc_al, acc_b, z_in, mine,
    tabs, tab_rx, tab_pair, tab_sum, tab_all, wide_s,
    tab_in, bias_s, attn_s, diff_s, qp_s, mi_s, mo_s, row_s, tab_s,
    hx_ss, hx_rs, hc_ss, hc_rs, back_ss, back_rs, pe_ss, pe_rs, pl_ss, pl_rs, ae_ss, ae_rs, al_ss, al_rs,
    be_ss, be_rs, bl_ss, bl_rs, z_ss, z_rs, g_ss, g_rs, t_ss, t_rs, tp_ss, tp_rs, tg_ss, tg_rs,
):
    lat = lax.axis_index("lat")
    lon = lax.axis_index("lon")
    core = lax.rem(lat, 2)
    zl = lat // 2
    zh = lon // 16
    plane = lax.rem(lon, 16)
    px = plane // 4
    py = lax.rem(plane, 4)
    at = functools.partial(neighbour, lat, lon, lats, lons)
    every = []

    def send(src, dst, ss, rs, device):
        copy = pltpu.make_async_remote_copy(
            src_ref=src, dst_ref=dst, send_sem=ss, recv_sem=rs, device_id=device, device_id_type=MESH
        )
        copy.start()
        every.append(copy)
        return copy

    barrier = pltpu.get_barrier_semaphore()

    def hello(device):
        pl.semaphore_signal(barrier, inc=1, device_id=device, device_id_type=MESH)

    hello(at(1, 1))
    hello(at(0, 1))
    hello(at(-1, -1))
    hello(at(0, -1))
    hello(at(1, 0))
    hello(at(-1, 0))
    for d in range(8):
        hello((lax.rem(lat + 2 * d, 16), lax.rem(lon + 16, 32)))
    for d in range(1, 16):
        hello((lax.rem(lat + d, 16), lon))
        hello((lat, zh * 16 + lax.rem(plane + d, 16)))

    attn_sample = 1 - keep[0, 0]
    sel_x[...] = fields[attn_sample]
    sel_c[...] = cotg[attn_sample]
    win_x[0:6, 0:3] = sel_x[6:12, 3:6]
    win_c[0:6, 0:3] = sel_c[6:12, 3:6]

    tab_in[...] = jnp.zeros(tab_in.shape, f32)
    for zn in range(2):
        for hn in range(12):
            spot = hn * 2 + 1 - zn
            for zm in range(2):
                start = ((zn * 2 + zm) * 12 + hn) * FLAT
                tab_in[spot * 8 : spot * 8 + HEADS, zm * FLAT : (zm + 1) * FLAT] = jnp.concatenate(
                    [table[h, :, start : start + FLAT] for h in range(HEADS)], axis=0
                )
    shifted = None
    for part in thirds(tab_in[...]):
        term = one(part, order[...], 1, 0)
        shifted = term if shifted is None else shifted + term
    for l in range(3):
        bias_s[l] = shifted[:, l * 128 : l * 128 + 128]

    marks = jnp.concatenate([region[w] for w in range(6)], axis=0).astype(bf16)
    pick = lax.broadcasted_iota(jnp.int32, (ZH, 12), 0) // 2 == lax.broadcasted_iota(jnp.int32, (ZH, 12), 1)
    marks = one(pick.astype(bf16), marks, 1, 1)
    lane12 = lax.broadcasted_iota(jnp.int32, (ZH, 12), 1)
    level = 1 - (lax.broadcasted_iota(jnp.int32, (ZH, 12), 0) & 1)
    columns = []
    for w in range(6):
        column = jnp.sum(jnp.where(lane12 == 2 * w + level, marks, 0.0), axis=1, keepdims=True)
        columns.append(jnp.broadcast_to(column, (ZH, TOK)))
    mark_rows = jnp.concatenate(columns, axis=0)
    same = mark_rows == mark_rows.T

    w_qkv = halves(wqkv[...])
    w_proj = halves(wproj[...])
    w_in = halves(win_w[...])
    w_out = halves(wout[...])

    pl.semaphore_wait(barrier, 6 + 30 + 8)
    halo_x = []
    halo_c = []
    for copies, src, dst, ss, rs in ((halo_x, sel_x, win_x, hx_ss, hx_rs), (halo_c, sel_c, win_c, hc_ss, hc_rs)):
        for slot, (sh, sw) in enumerate(((0, 0), (1, 0), (0, 1))):
            copies.append(
                send(
                    src.at[pl.ds(sh * 6, 6), pl.ds(sw * 3, 3)],
                    dst.at[pl.ds(6 - sh * 6, 6), pl.ds(3 - sw * 3, 3)],
                    ss.at[slot], rs.at[slot],
                    at(sh - 1, sw - 1),
                )
            )
    for copy in halo_x:
        copy.wait_recv()

    x = take_tokens(lambda w: win_x[:, w])
    unit1, inv1 = norm_parts(x)
    gain1 = n1g[...].reshape(1, C)
    normed1 = halves(unit1 * gain1 + n1s[...].reshape(1, C))
    proj = product(normed1, w_qkv) + bqkv[...].reshape(1, 3 * C)
    query = halves(proj[:, 0:C] * scale)
    key = halves(proj[:, C : 2 * C])
    value = halves(proj[:, 2 * C : 3 * C])
    lanes = lax.broadcasted_iota(jnp.int32, (1, C), 1)
    masks = [(lanes // 32 == h) for h in range(HEADS)]

    def masked(pair, h):
        zero = jnp.zeros((), bf16)
        return tuple(jnp.where(masks[h], part, zero) for part in pair)

    mixed = jnp.zeros((TOK, C), f32)
    for h in range(HEADS):
        scores = product(masked(query, h), key, 1, 1)
        strip = jnp.concatenate([bias_s[l, pl.ds(h, ZH, stride=8), :] for l in range(3)], axis=1)
        bias = jnp.concatenate(
            [pltpu.roll(strip, (384 - (5 - wn) * ZH) % 384, axis=1)[:, 0:TOK] for wn in range(6)], axis=0
        )
        scores = jnp.where(same, scores + bias, -1e30)
        scores = jnp.exp(scores - jnp.max(scores, axis=-1, keepdims=True))
        attn = scores / jnp.sum(scores, axis=-1, keepdims=True)
        attn_s[h] = attn
        mixed = mixed + product(halves(attn), masked(value, h))
    mixed = halves(mixed)
    branch = product(mixed, w_proj) + bproj[...].reshape(1, C)

    for copy in halo_c:
        copy.wait_recv()
    cot = take_tokens(lambda w: win_c[:, w])
    both = keep[0, 0] == keep[0, 1]
    loc_x = take_tokens(lambda w: fields[1 - attn_sample, :, w])
    loc_cot = take_tokens(lambda w: cotg[1 - attn_sample, :, w])
    middle = jnp.where(both, x + kept * branch, loc_x)
    cot_m = jnp.where(both, cot, loc_cot)
    unit2, inv2 = norm_parts(middle)
    gain2 = n2g[...].reshape(1, C)
    normed2 = halves(unit2 * gain2 + n2s[...].reshape(1, C))
    hidden = product(normed2, w_in) + b_in[...].reshape(1, HID)
    cdf = 0.5 * (1.0 + lax.erf(hidden * math.sqrt(0.5)))
    slope = cdf + hidden * jnp.exp(-0.5 * hidden * hidden) * (1.0 / math.sqrt(2.0 * math.pi))
    grad_y = halves(kept * cot_m)
    grad_hidden = halves(product(grad_y, w_out) * slope)
    mo_s[:, 0:C] = product(halves(hidden * cdf), grad_y, 0, 0)

    ones_lane = (lax.broadcasted_iota(jnp.int32, (1, 256), 1) & 7) == 6

    def spread_out(pair):
        high = one(pair[0], spread[...], 1, 0)
        low = one(pair[1], spread[...], 1, 0)
        return jnp.where(ones_lane, 1.0, high).astype(bf16), low.astype(bf16)

    mi_s[...] = product(spread_out(normed2), grad_hidden, 0, 0)

    low_lanes = lax.broadcasted_iota(jnp.int32, (8, 128), 1) < 64

    def put(buffer, count, j, tile_id, tile, rows=slice(None)):
        a = lax.rem(j // 4, 4)
        b = lax.rem(j, 4)
        if tile_id < count:
            buffer[0, a, b, j // 16, tile_id, rows, :] = tile
        else:
            buffer[1, b, a, j // 16, tile_id - count, rows, :] = tile

    def pack_early(j, carry):
        at8 = pl.ds(pl.multiple_of(j * 8, 8), 8)
        for t in range(6):
            put(early, 5, j, t, mi_s[at8, t * 128 : t * 128 + 128])
        tails = []
        for k in range(3):
            rows = pl.ds(pl.multiple_of(j * 24 + k * 8, 8), 8)
            put(early, 5, j, 6 + k, mo_s[rows, 0:128])
            tails.append(mo_s[rows, 128:256])
        put(early, 5, j, 9, jnp.where(low_lanes, tails[0], pltpu.roll(tails[1], 64, axis=1)))
        pairs = jnp.where(low_lanes, tails[2], pltpu.roll(pltpu.roll(tails[2], 64, axis=1), 7, axis=0))
        for k in range(4):
            put(early, 5, j, k, pairs[2 * k : 2 * k + 1, :], slice(7, 8))
        return carry

    lax.fori_loop(0, 32, pack_early, 0)
    twin = (lat + 1 - 2 * core, lon)
    pair_early = send(early.at[1 - core], pair_e, pe_ss, pe_rs, twin)

    grad_n2 = product(grad_hidden, w_in, 1, 1)
    row_s[0:1, 2 * C : 3 * C] = jnp.sum(grad_n2 * unit2, axis=0, keepdims=True)
    row_s[0:1, 3 * C : 4 * C] = jnp.sum(grad_n2, axis=0, keepdims=True)
    grad_m = cot_m + norm_back(grad_n2, gain2, unit2, inv2)
    grad_a = jnp.where(both, grad_m, cot)

    def put_other(w, block):
        other[:, w] = block

    put_tokens(put_other, jnp.where(both, loc_cot, grad_m))

    first = px + core * (py - px)
    second = py + core * (px - py)

    def along(pos_first, pos_second):
        x_pos = pos_first + core * (pos_second - pos_first)
        y_pos = pos_second + core * (pos_first - pos_second)
        return lat, zh * 16 + x_pos * 4 + y_pos

    def add_pair(buffer, arrived):
        def step(i, carry):
            for j in range(4):
                arrived[i, j] = arrived[i, j] + buffer[core, i, j]
            return carry

        lax.fori_loop(0, 4, step, 0)

    def send_first(arrived, slots, ss, rs):
        copies = []
        for d in range(1, 4):
            to = lax.rem(first + d, 4)
            copies.append(send(arrived.at[to], slots.at[d - 1], ss.at[d - 1], rs.at[d - 1], along(to, second)))
        return copies

    def add_first(arrived, slots, acc):
        for j in range(4):
            acc[j] = (arrived[first, j] + slots[0, j]) + (slots[1, j] + slots[2, j])

    def send_second(acc, slots, ss, rs):
        copies = []
        for d in range(1, 4):
            to = lax.rem(second + d, 4)
            copies.append(send(acc.at[to], slots.at[d - 1], ss.at[d - 1], rs.at[d - 1], along(first, to)))
        return copies

    grad_b = halves(kept * grad_a)
    qp_s[:, 3 * C : 4 * C] = product(spread_out(mixed), grad_b, 0, 0)
    grad_o = halves(product(grad_b, w_proj, 1, 1))
    grad_q = jnp.zeros((TOK, C), f32)
    grad_k = jnp.zeros((TOK, C), f32)
    grad_v = jnp.zeros((TOK, C), f32)
    diff_s[...] = jnp.zeros(diff_s.shape, f32)
    first_early = None
    for h in range(HEADS):
        attn = attn_s[h]
        grad_oh = masked(grad_o, h)
        grad_attn = product(grad_oh, value, 1, 1)
        grad_v = grad_v + product(halves(attn), grad_oh, 0, 0)
        term = attn * grad_attn
        grad_s = term - attn * jnp.sum(term, axis=-1, keepdims=True)
        grad_sp = halves(grad_s)
        grad_q = grad_q + product(grad_sp, masked(key, h))
        grad_k = grad_k + product(grad_sp, masked(query, h), 0, 0)
        wide = jnp.concatenate([grad_s, jnp.zeros((TOK, 384 - TOK), f32)], axis=1)
        total = None
        for wn in range(6):
            block = wide[wn * ZH : (wn + 1) * ZH, :]
            if wn < 5:
                block = pltpu.roll(block, (5 - wn) * ZH, axis=1)
            total = block if total is None else total + block
        for l in range(3):
            diff_s[l, pl.ds(h, ZH, stride=8), :] = total[:, l * 128 : l * 128 + 128]
        if h == 1:
            pair_early.wait_recv()
            add_pair(early, pair_e)
            first_early = send_first(pair_e, a_e, ae_ss, ae_rs)
    grad_p = halves(jnp.concatenate([grad_q * scale, grad_k, grad_v], axis=1))
    qp_s[:, 0 : 3 * C] = product(spread_out(normed1), grad_p, 0, 0)
    grad_n1 = product(grad_p, w_qkv, 1, 1)
    row_s[0:1, 0:C] = jnp.sum(grad_n1 * unit1, axis=0, keepdims=True)
    row_s[0:1, C : 2 * C] = jnp.sum(grad_n1, axis=0, keepdims=True)

    def pack_late(j, carry):
        at8 = pl.ds(pl.multiple_of(j * 8, 8), 8)
        last = lax.broadcasted_iota(jnp.int32, (8, 128), 0) == 7
        for t in range(6):
            part = slice(t * 128, t * 128 + 128)
            put(late, 3, j, t, jnp.where(last, row_s[0:1, part], qp_s[at8, part]))
        return carry

    lax.fori_loop(0, 32, pack_late, 0)
    pair_late = send(late.at[1 - core], pair_l, pl_ss, pl_rs, twin)

    grad_x = grad_a + norm_back(grad_n1, gain1, unit1, inv1)

    def put_dxa(w, block):
        dxa[:, w] = block

    put_tokens(put_dxa, grad_x)
    home = []
    for slot, (hh, wh) in enumerate(((1, 1), (0, 1), (1, 0))):
        home.append(
            send(
                dxa.at[pl.ds(hh * 6, 6), pl.ds(wh * 3, 3)],
                back.at[pl.ds(6 - hh * 6, 6), pl.ds(3 - wh * 3, 3)],
                back_ss.at[slot], back_rs.at[slot], at(hh, wh),
            )
        )
    back[6:12, 3:6] = dxa[0:6, 0:3]

    diff = halves(jnp.concatenate([diff_s[l] for l in range(3)], axis=1))
    lanes_back = one(diff[0], order[...], 1, 1) + one(diff[1], order[...], 1, 1)
    tail = one(diff[0], rest[...], 1, 0) + one(diff[1], rest[...], 1, 0)
    row_id = lax.broadcasted_iota(jnp.int32, tail.shape, 0) & 7
    lane_id = lax.broadcasted_iota(jnp.int32, tail.shape, 1) // 8
    tail = jnp.where(row_id == lane_id, tail, 0.0).reshape(ZH, 8, 128).sum(axis=1)
    for l in range(2):
        tab_s[l] = lanes_back[:, l * 128 : l * 128 + 128]
    tab_s[0, pl.ds(6, ZH, stride=8), :] = tail
    for k in range(8):
        for l in range(2):
            tabs[2 * k + l] = tab_s[l, 24 * k : 24 * k + 24, :]

    pair_late.wait_recv()
    add_pair(late, pair_l)
    first_late = send_first(pair_l, a_l, al_ss, al_rs)
    tab_copies = []
    for d in range(1, 16):
        to = lax.rem(plane + d, 16)
        tab_copies.append(send(tabs.at[to], tab_rx.at[d - 1], t_ss.at[d - 1], t_rs.at[d - 1], (lat, zh * 16 + to)))

    for copy in first_early:
        copy.wait_recv()
    add_first(pair_e, a_e, acc_ae)
    second_early = send_second(acc_ae, b_e, be_ss, be_rs)

    for copy in first_late:
        copy.wait_recv()
    add_first(pair_l, a_l, acc_al)
    second_late = send_second(acc_al, b_l, bl_ss, bl_rs)

    for copy in tab_copies:
        copy.wait_recv()
    total = tabs[plane]
    for d in range(15):
        total = total + tab_rx[d]
    tab_sum[...] = total
    tab_across = send(tab_sum, tab_pair, tp_ss, tp_rs, (lat, lax.rem(lon + 16, 32)))

    for copy in second_early:
        copy.wait_recv()
    acc_b[:, 3:8] = (acc_ae[second] + b_e[0]) + (b_e[1] + b_e[2])
    for copy in second_late:
        copy.wait_recv()
    acc_b[:, 0:3] = (acc_al[second] + b_l[0]) + (b_l[1] + b_l[2])
    z_copies = []
    for d in (8, 7, 9, 6, 10, 5, 11, 4, 12, 3, 13, 2, 14, 1, 15):
        to = lax.rem(zh * 8 + zl + d, 16)
        z_copies.append(
            send(
                acc_b.at[to // 8, lax.rem(to, 8)], z_in.at[d - 1], z_ss.at[d - 1], z_rs.at[d - 1],
                (lax.rem(to, 8) * 2 + core, (to // 8) * 16 + plane),
            )
        )

    tab_across.wait_recv()
    tab_all[plane] = tab_sum[...] + tab_pair[...]
    tab_back = []
    for d in range(1, 16):
        to = lax.rem(plane + d, 16)
        tab_back.append(
            send(tab_all.at[plane], tab_all.at[plane], tg_ss.at[d - 1], tg_rs.at[d - 1], (lat, zh * 16 + to))
        )

    for copy in z_copies:
        copy.wait_recv()
    total = acc_b[zh, zl]
    for d in range(15):
        total = total + z_in[d]
    slot = core * 8 + zl
    mine[...] = total
    gather[slot] = total
    g_copies = []
    for d in range(1, 16):
        to = lax.rem(lat + d, 16)
        g_copies.append(send(mine, gather.at[slot], g_ss.at[d - 1], g_rs.at[d - 1], (to, lon)))

    for copy in tab_back:
        copy.wait_recv()
    for k in range(8):
        for l in range(2):
            wide_s[l, 24 * k : 24 * k + 24, :] = tab_all[2 * k + l]
    tail = wide_s[0, pl.ds(6, ZH, stride=8), :]
    for h in range(HEADS):
        moved = tail if h == 0 else pltpu.roll(tail, 128 - 8 * h, axis=1)
        wide_s[2, pl.ds(h, ZH, stride=8), :] = moved
    for zn in range(2):
        for hn in range(12):
            spot = hn * 2 + 1 - zn
            block = jnp.concatenate([wide_s[l, spot * 8 : spot * 8 + 8, :] for l in range(3)], axis=1)
            for zm in range(2):
                start = ((zn * 2 + zm) * 12 + hn) * FLAT
                for h in range(HEADS):
                    table_o[h, :, start : start + FLAT] = block[h : h + 1, zm * FLAT : (zm + 1) * FLAT]

    for copy in home:
        copy.wait_recv()
    for copy in g_copies:
        copy.wait_recv()
    for copy in every:
        copy.wait_send()


def kernel_b(
    keep, gather, table_i, back, other,
    fields_grad, n1g_o, n1s_o, qkvw_o, qkvb_o, table_o, projw_o, projb_o, n2g_o, n2s_o, inw_o, inb_o, outw_o,
):
    table_o[...] = table_i[...]
    first_kept = keep[0, 0] == 1
    fields_grad[0] = jnp.where(first_kept, back[...], other[...])
    fields_grad[1] = jnp.where(first_kept, other[...], back[...])

    def late(t):
        return gather.at[(t // 3) * 8 + t % 3]

    def early(t):
        return gather.at[(t // 5) * 8 + 3 + t % 5]

    def strip(tile, row, rows):
        return jnp.concatenate([tile(t)[row : row + rows, :] for t in range(6)], axis=1)

    sums = strip(late, 0, 6)
    qkvw_o[...] = sums[:, 0 : 3 * C]
    projw_o[...] = sums[:, 3 * C : 4 * C]
    inw_o[...] = strip(early, 0, 6)
    small = strip(late, 6, 1)
    qkvb_o[...] = small[:, 0 : 3 * C].reshape(3 * C)
    projb_o[...] = small[:, 3 * C : 4 * C].reshape(C)
    inb_o[...] = strip(early, 6, 1).reshape(HID)
    norms = strip(late, 7, 1)
    for i, ref in enumerate((n1g_o, n1s_o, n2g_o, n2s_o)):
        ref[...] = norms[:, i * C : (i + 1) * C].reshape(C)
    for k in range(3):
        outw_o[8 * k : 8 * k + 8, 0:128] = early(6 + k)[...]
    mix = early(9)[...]
    outw_o[0:8, 128:192] = mix[:, 0:64]
    outw_o[8:16, 128:192] = pltpu.roll(mix, 64, axis=1)[:, 0:64]
    for k in range(4):
        line = early(k)[7:8, :]
        outw_o[16 + 2 * k : 17 + 2 * k, 128:192] = line[:, 0:64]
        outw_o[17 + 2 * k : 18 + 2 * k, 128:192] = pltpu.roll(line, 64, axis=1)[:, 0:64]


def shape(*dims):
    return jax.ShapeDtypeStruct(dims, f32)


def vmem():
    return pl.BlockSpec(memory_space=pltpu.VMEM)


def smem():
    return pl.BlockSpec(memory_space=pltpu.SMEM)


def per_device(lats, lons, fields, cotangent, keep_mask, region_ids, *weights):
    order, rest = (jnp.asarray(m, bf16) for m in bias_order())
    spread = jnp.asarray(spread_order(), bf16)
    weights = list(weights)
    weights[4] = weights[4].transpose(1, 0, 2)
    weights[-1] = weights[-1].T
    grid_order = (0, 2, 3, 1, 4)
    one_sem = pltpu.SemaphoreType.DMA

    def sems(count):
        return pltpu.SemaphoreType.DMA((count,))

    def buf(*dims):
        return pltpu.VMEM(dims, f32)

    tile = (8, 128)
    block = (12, 6, 2, C)
    packed = pl.pallas_call(
        functools.partial(kernel_a, lats, lons),
        out_shape=(shape(16, 8, 128), shape(*(HEADS, 1, 6336)), shape(*block), shape(*block)),
        in_specs=[smem()] + [vmem()] * 18,
        out_specs=(vmem(),) * 4,
        scratch_shapes=[
            buf(*block), buf(*block), buf(*block), buf(*block), buf(*block),
            buf(2, 4, 4, 2, 5, *tile), buf(2, 4, 4, 2, 3, *tile),
            buf(4, 4, 2, 5, *tile), buf(4, 4, 2, 3, *tile),
            buf(3, 4, 2, 5, *tile), buf(3, 4, 2, 3, *tile),
            buf(3, 2, 5, *tile), buf(3, 2, 3, *tile),
            buf(4, 2, 5, *tile), buf(4, 2, 3, *tile),
            buf(2, 8, *tile), buf(15, *tile), buf(*tile),
            buf(16, 24, 128), buf(15, 24, 128), buf(24, 128), buf(24, 128), buf(16, 24, 128), buf(3, 192, 128),
            buf(192, 384), buf(3, 192, 128), buf(HEADS, TOK, TOK), buf(3, 192, 128),
            buf(256, 768), buf(256, 768), buf(768, 256), buf(8, 768), buf(2, 192, 128),
            sems(3), sems(3), sems(3), sems(3), sems(3), sems(3),
            one_sem, one_sem, one_sem, one_sem,
            sems(3), sems(3), sems(3), sems(3), sems(3), sems(3), sems(3), sems(3),
            sems(15), sems(15), sems(15), sems(15), sems(15), sems(15), one_sem, one_sem, sems(15), sems(15),
        ],
        compiler_params=pltpu.CompilerParams(collective_id=0, has_side_effects=True, vmem_limit_bytes=VMEM_LIMIT),
        name="block_both_ways",
    )(
        keep_mask, fields.transpose(grid_order), cotangent.transpose(grid_order), region_ids.transpose(2, 0, 1),
        *weights, order, rest, spread,
    )
    outs = list(
        pl.pallas_call(
            kernel_b,
            out_shape=(
                shape(2, *block), shape(C), shape(C), shape(6, 3 * C), shape(3 * C), shape(*(HEADS, 1, 6336)),
                shape(6, C), shape(C), shape(C), shape(C), shape(6, HID), shape(HID), shape(24, C),
            ),
            in_specs=[smem()] + [vmem()] * 4,
            out_specs=(vmem(),) * 13,
            compiler_params=pltpu.CompilerParams(vmem_limit_bytes=VMEM_LIMIT),
            name="unpack",
        )(keep_mask, *packed)
    )
    outs[0] = outs[0].transpose(0, 3, 1, 2, 4)
    outs[5] = outs[5].transpose(1, 0, 2)
    return tuple(outs)


def solution(mesh):
    grid = P(None, None, "lat", "lon", None)
    rows = P("lon", None)
    return jax.shard_map(
        functools.partial(per_device, mesh.shape["lat"], mesh.shape["lon"]),
        mesh=mesh,
        in_specs=(grid, grid, P(), P(None, "lat", "lon"), P(), P(), P(), P(), P("lat", None, None))
        + (P(),) * 7,
        out_specs=(grid, P(), P(), rows, P(), P("lat", None, None), rows, P(), P(), P(), rows, P(), rows),
        check_vma=False,
    )
```

```python
import functools
import math

import jax
import jax.numpy as jnp
import numpy as np
from jax import lax
from jax.experimental import pallas as pl
from jax.experimental.pallas import tpu as pltpu
from jax.sharding import PartitionSpec as P

f32 = jnp.float32
bf16 = jnp.bfloat16
MESH = pl.DeviceIdType.MESH
C = 192
HEADS = 6
HID = 768
TOK = 144
ZH = 24
REL = 11
FLAT = 132
eps = 1e-05
kept = 1.25
scale = 1.0 / math.sqrt(32.0)
VMEM_LIMIT = 56 * 1024 * 1024


def bias_order():
    to = np.zeros((384, 384), np.float32)
    rest = np.zeros((384, 128), np.float32)
    for z in range(2):
        for h in range(12):
            for r in range(REL):
                lane = z * FLAT + h * REL + r
                spot = (REL - 1 - r) * ZH + h * 2 + 1 - z
                to[lane, spot] = 1.0
                if lane >= 256:
                    for head in range(HEADS):
                        rest[spot, 8 * head + lane - 256] = 1.0
    return to, rest


def spread_order():
    to = np.zeros((C, 256), np.float32)
    for feature in range(C):
        to[feature, 8 * (feature // 6) + feature % 6] = 1.0
    return to


def halves(values):
    high = values.astype(bf16)
    return high, (values - high.astype(f32)).astype(bf16)


def thirds(values):
    high = values.astype(bf16)
    left = values - high.astype(f32)
    mid = left.astype(bf16)
    return high, mid, (left - mid.astype(f32)).astype(bf16)


def one(a, b, ca, cb):
    return lax.dot_general(a, b, (((ca,), (cb,)), ((), ())), preferred_element_type=f32)


def product(a, b, ca=1, cb=0):
    return one(a[0], b[0], ca, cb) + (one(a[0], b[1], ca, cb) + one(a[1], b[0], ca, cb))


def norm_parts(values):
    center = values - jnp.mean(values, axis=-1, keepdims=True)
    spread = jnp.mean(center * center, axis=-1, keepdims=True)
    inv = lax.rsqrt(spread + eps)
    return center * inv, inv


def norm_back(grad, gain, unit, inv):
    scaled = grad * gain
    return inv * (
        scaled
        - jnp.mean(scaled, axis=-1, keepdims=True)
        - unit * jnp.mean(scaled * unit, axis=-1, keepdims=True)
    )


def neighbour(lat, lon, lats, lons, dlat, dlon):
    return lax.rem(lat + dlat + lats, lats), lax.rem(lon + dlon + lons, lons)


def take_tokens(read):
    return jnp.concatenate([read(w).reshape(ZH, C) for w in range(6)], axis=0)


def put_tokens(write, values):
    for w in range(6):
        write(w, values[w * ZH : (w + 1) * ZH, :].reshape(12, 2, C))


def kernel_a(
    lats, lons,
    keep, *refs,
):
    hbm, refs = refs[0:18], refs[18:]
    results, refs = refs[0:4], refs[4:]
    loaded, refs = refs[0:18], refs[18:]
    compute_and_sum(lats, lons, keep, hbm, loaded, *results, *loaded, *refs)


def compute_and_sum(
    lats, lons, keep, hbm, loaded,
    gather, table_o, back, other,
    fields, cotg, region, n1g, n1s, wqkv, bqkv, table, wproj, bproj, n2g, n2s, win_w, b_in, wout,
    order, rest, spread,
    load_sem, sel_x, sel_c, win_x, win_c, dxa, region_win,
    early, late, pair_e, pair_l, a_e, a_l, b_e, b_l, acc_ae, acc_al, acc_b, z_in, mine,
    tabs, tab_rx, tab_pair, tab_sum, tab_all, wide_s,
    tab_in, bias_s, attn_s, diff_s, qp_s, row_s, tab_s,
    hx_ss, hx_rs, hc_ss, hc_rs, reg_ss, reg_rs, back_ss, back_rs, pe_ss, pe_rs, pl_ss, pl_rs, ae_ss, ae_rs, al_ss, al_rs,
    be_ss, be_rs, bl_ss, bl_rs, z_ss, z_rs, g_ss, g_rs, t_ss, t_rs, tp_ss, tp_rs, tg_ss, tg_rs,
):
    lat = lax.axis_index("lat")
    lon = lax.axis_index("lon")
    core = lax.rem(lat, 2)
    zl = lat // 2
    zh = lon // 16
    plane = lax.rem(lon, 16)
    px = plane // 4
    py = lax.rem(plane, 4)
    at = functools.partial(neighbour, lat, lon, lats, lons)
    every = []

    def send(src, dst, ss, rs, device):
        copy = pltpu.make_async_remote_copy(
            src_ref=src, dst_ref=dst, send_sem=ss, recv_sem=rs, device_id=device, device_id_type=MESH
        )
        copy.start()
        every.append(copy)
        return copy

    barrier = pltpu.get_barrier_semaphore()

    def hello(device):
        pl.semaphore_signal(barrier, inc=1, device_id=device, device_id_type=MESH)

    hello(at(1, -1))
    hello(at(0, -1))
    hello(at(-1, 1))
    hello(at(0, 1))
    hello(at(1, 0))
    hello(at(-1, 0))
    for d in range(0, 16, 2):
        hello((lax.rem(lat + d, 16), lax.rem(lon + 16, 32)))
    for d in range(1, 16):
        hello((lax.rem(lat + d, 16), lon))
        hello((lat, zh * 16 + lax.rem(plane + d, 16)))

    loads = [pltpu.make_async_copy(hbm[i], loaded[i], load_sem.at[i]) for i in range(18)]
    for i in (0, 1, 7, 15, 2, 5, 8, 12, 14, 16, 17, 3, 4, 6, 9, 10, 11, 13):
        loads[i].start()
    attn_sample = 1 - keep[0, 0]
    loads[0].wait()
    loads[1].wait()
    sel_x[...] = fields[attn_sample]
    sel_c[...] = cotg[attn_sample]
    win_x[0:6, 3:6] = sel_x[6:12, 0:3]
    win_c[0:6, 3:6] = sel_c[6:12, 0:3]

    halo_x = []
    halo_c = []
    quadrants = ((0, 1), (1, 1), (0, 0))

    def start_halo(src, dst, ss, rs, copies):
        for slot, (sh, sw) in enumerate(quadrants):
            copies.append(
                send(
                    src.at[pl.ds(sh * 6, 6), pl.ds(sw * 3, 3)],
                    dst.at[pl.ds(6 - sh * 6, 6), pl.ds(3 - sw * 3, 3)],
                    ss.at[slot], rs.at[slot], at(sh - 1, sw),
                )
            )

    pl.semaphore_wait(barrier, 6 + 30 + 8)
    start_halo(sel_x, win_x, hx_ss, hx_rs, halo_x)
    loads[2].wait()
    regions = send(region, region_win, reg_ss, reg_rs, at(0, 1))

    for i in (7, 15):
        loads[i].wait()

    tab_in[...] = jnp.zeros(tab_in.shape, f32)
    for zn in range(2):
        for hn in range(12):
            spot = hn * 2 + 1 - zn
            for zm in range(2):
                start = ((zn * 2 + zm) * 12 + hn) * FLAT
                tab_in[spot * 8 : spot * 8 + HEADS, zm * FLAT : (zm + 1) * FLAT] = jnp.concatenate(
                    [table[h, :, start : start + FLAT] for h in range(HEADS)], axis=0
                )
    shifted = None
    for part in thirds(tab_in[...]):
        term = one(part, order[...], 1, 0)
        shifted = term if shifted is None else shifted + term
    for l in range(3):
        bias_s[l] = shifted[:, l * 128 : l * 128 + 128]

    for i in (5, 8, 12, 14, 16, 17, 3, 4, 6, 9, 10, 11, 13):
        loads[i].wait()
    w_qkv = halves(wqkv[...])
    w_proj = halves(wproj[...])
    w_in = halves(win_w[...])
    w_out = halves(wout[...])

    loc_x = take_tokens(lambda w: fields[1 - attn_sample, :, w])
    loc_cot = take_tokens(lambda w: cotg[1 - attn_sample, :, w])
    start_halo(sel_c, win_c, hc_ss, hc_rs, halo_c)

    regions.wait_recv()
    marks = jnp.concatenate([region_win[w] for w in range(6)], axis=0).astype(bf16)
    pick = lax.broadcasted_iota(jnp.int32, (ZH, 12), 0) // 2 == lax.broadcasted_iota(jnp.int32, (ZH, 12), 1)
    marks = one(pick.astype(bf16), marks, 1, 1)
    lane12 = lax.broadcasted_iota(jnp.int32, (ZH, 12), 1)
    level = 1 - (lax.broadcasted_iota(jnp.int32, (ZH, 12), 0) & 1)
    columns = []
    for w in range(6):
        column = jnp.sum(jnp.where(lane12 == 2 * w + level, marks, 0.0), axis=1, keepdims=True)
        columns.append(jnp.broadcast_to(column, (ZH, TOK)))
    mark_rows = jnp.concatenate(columns, axis=0)
    same = mark_rows == mark_rows.T

    for copy in halo_x:
        copy.wait_recv()

    x = take_tokens(lambda w: win_x[:, w])
    unit1, inv1 = norm_parts(x)
    gain1 = n1g[...].reshape(1, C)
    normed1 = halves(unit1 * gain1 + n1s[...].reshape(1, C))
    proj = product(normed1, w_qkv) + bqkv[...].reshape(1, 3 * C)
    query = halves(proj[:, 0:C] * scale)
    key = halves(proj[:, C : 2 * C])
    value = halves(proj[:, 2 * C : 3 * C])
    lanes = lax.broadcasted_iota(jnp.int32, (1, C), 1)
    masks = [(lanes // 32 == h) for h in range(HEADS)]

    def masked(pair, h):
        zero = jnp.zeros((), bf16)
        return tuple(jnp.where(masks[h], part, zero) for part in pair)

    mixed = jnp.zeros((TOK, C), f32)
    for h in range(HEADS):
        scores = product(masked(query, h), key, 1, 1)
        strip = jnp.concatenate([bias_s[l, pl.ds(h, ZH, stride=8), :] for l in range(3)], axis=1)
        bias = jnp.concatenate(
            [pltpu.roll(strip, (384 - (5 - wn) * ZH) % 384, axis=1)[:, 0:TOK] for wn in range(6)], axis=0
        )
        scores = jnp.where(same, scores + bias, -1e30)
        scores = jnp.exp(scores - jnp.max(scores, axis=-1, keepdims=True))
        attn = scores / jnp.sum(scores, axis=-1, keepdims=True)
        attn_s[h] = attn
        mixed = mixed + product(halves(attn), masked(value, h))
    mixed = halves(mixed)
    branch = product(mixed, w_proj) + bproj[...].reshape(1, C)

    for copy in halo_c:
        copy.wait_recv()
    cot = take_tokens(lambda w: win_c[:, w])
    both = keep[0, 0] == keep[0, 1]
    middle = jnp.where(both, x + kept * branch, loc_x)
    cot_m = jnp.where(both, cot, loc_cot)
    unit2, inv2 = norm_parts(middle)
    gain2 = n2g[...].reshape(1, C)
    normed2 = halves(unit2 * gain2 + n2s[...].reshape(1, C))
    hidden = product(normed2, w_in) + b_in[...].reshape(1, HID)
    cdf = 0.5 * (1.0 + lax.erf(hidden * math.sqrt(0.5)))
    slope = cdf + hidden * jnp.exp(-0.5 * hidden * hidden) * (1.0 / math.sqrt(2.0 * math.pi))
    grad_y = halves(kept * cot_m)
    grad_hidden = halves(product(grad_y, w_out) * slope)
    grad_out_w = product(halves(hidden * cdf), grad_y, 0, 0)

    ones_lane = (lax.broadcasted_iota(jnp.int32, (1, 256), 1) & 7) == 6

    def spread_out(pair):
        high = one(pair[0], spread[...], 1, 0)
        low = one(pair[1], spread[...], 1, 0)
        return jnp.where(ones_lane, 1.0, high).astype(bf16), low.astype(bf16)

    grad_in_w = product(spread_out(normed2), grad_hidden, 0, 0)

    low_lanes = lax.broadcasted_iota(jnp.int32, (8, 128), 1) < 64

    def put(buffer, count, j, tile_id, tile, rows=slice(None)):
        zh_j, a, b = j // 16, j // 4 % 4, j % 4
        if tile_id < count:
            buffer[0, a, b, zh_j, tile_id, rows, :] = tile
        else:
            buffer[1, b, a, zh_j, tile_id - count, rows, :] = tile

    last_row = lax.broadcasted_iota(jnp.int32, (8, 128), 0) == 7
    for j in range(32):
        block = grad_out_w[24 * j : 24 * j + 24, :]
        tails = [
            jnp.concatenate([block[8 * k : 8 * k + 8, 128:192], jnp.zeros((8, 64), f32)], axis=1) for k in range(3)
        ]
        for k in range(3):
            put(early, 5, j, 6 + k, block[8 * k : 8 * k + 8, 0:128])
        put(early, 5, j, 9, tails[0] + pltpu.roll(tails[1], 64, axis=1))
        pairs = tails[2] + pltpu.roll(pltpu.roll(tails[2], 64, axis=1), 7, axis=0)
        for t in range(6):
            tile = grad_in_w[8 * j : 8 * j + 8, t * 128 : t * 128 + 128]
            if t < 4:
                tile = jnp.where(last_row, pairs[2 * t : 2 * t + 1, :], tile)
            put(early, 5, j, t, tile)
    twin = (lat + 1 - 2 * core, lon)
    pair_early = send(early.at[1 - core], pair_e, pe_ss, pe_rs, twin)

    grad_n2 = product(grad_hidden, w_in, 1, 1)
    row_s[0:1, 2 * C : 3 * C] = jnp.sum(grad_n2 * unit2, axis=0, keepdims=True)
    row_s[0:1, 3 * C : 4 * C] = jnp.sum(grad_n2, axis=0, keepdims=True)
    grad_m = cot_m + norm_back(grad_n2, gain2, unit2, inv2)
    grad_a = jnp.where(both, grad_m, cot)

    def put_other(w, block):
        other[:, w] = block

    put_tokens(put_other, jnp.where(both, loc_cot, grad_m))

    first = px + core * (py - px)
    second = py + core * (px - py)

    def along(pos_first, pos_second):
        x_pos = pos_first + core * (pos_second - pos_first)
        y_pos = pos_second + core * (pos_first - pos_second)
        return lat, zh * 16 + x_pos * 4 + y_pos

    def add_pair(buffer, arrived):
        for i in range(4):
            for j in range(4):
                arrived[i, j] = arrived[i, j] + buffer[core, i, j]

    def send_first(arrived, slots, ss, rs):
        copies = []
        for d in range(1, 4):
            to = lax.rem(first + d, 4)
            copies.append(send(arrived.at[to], slots.at[d - 1], ss.at[d - 1], rs.at[d - 1], along(to, second)))
        return copies

    def add_first(arrived, slots, acc):
        for j in range(4):
            acc[j] = (arrived[first, j] + slots[0, j]) + (slots[1, j] + slots[2, j])

    def send_second(acc, slots, ss, rs):
        copies = []
        for d in range(1, 4):
            to = lax.rem(second + d, 4)
            copies.append(send(acc.at[to], slots.at[d - 1], ss.at[d - 1], rs.at[d - 1], along(first, to)))
        return copies

    grad_b = halves(kept * grad_a)
    qp_s[:, 3 * C : 4 * C] = product(spread_out(mixed), grad_b, 0, 0)
    grad_o = halves(product(grad_b, w_proj, 1, 1))
    grad_q = jnp.zeros((TOK, C), f32)
    grad_k = jnp.zeros((TOK, C), f32)
    grad_v = jnp.zeros((TOK, C), f32)
    diff_s[...] = jnp.zeros(diff_s.shape, f32)
    first_early = None
    for h in range(HEADS):
        attn = attn_s[h]
        grad_oh = masked(grad_o, h)
        grad_attn = product(grad_oh, value, 1, 1)
        grad_v = grad_v + product(halves(attn), grad_oh, 0, 0)
        term = attn * grad_attn
        grad_s = term - attn * jnp.sum(term, axis=-1, keepdims=True)
        grad_sp = halves(grad_s)
        grad_q = grad_q + product(grad_sp, masked(key, h))
        grad_k = grad_k + product(grad_sp, masked(query, h), 0, 0)
        wide = jnp.concatenate([grad_s, jnp.zeros((TOK, 384 - TOK), f32)], axis=1)
        total = None
        for wn in range(6):
            block = wide[wn * ZH : (wn + 1) * ZH, :]
            if wn < 5:
                block = pltpu.roll(block, (5 - wn) * ZH, axis=1)
            total = block if total is None else total + block
        for l in range(3):
            diff_s[l, pl.ds(h, ZH, stride=8), :] = total[:, l * 128 : l * 128 + 128]
        if h == 1:
            pair_early.wait_recv()
            add_pair(early, pair_e)
            first_early = send_first(pair_e, a_e, ae_ss, ae_rs)
    grad_p = halves(jnp.concatenate([grad_q * scale, grad_k, grad_v], axis=1))
    qp_s[:, 0 : 3 * C] = product(spread_out(normed1), grad_p, 0, 0)
    grad_n1 = product(grad_p, w_qkv, 1, 1)
    row_s[0:1, 0:C] = jnp.sum(grad_n1 * unit1, axis=0, keepdims=True)
    row_s[0:1, C : 2 * C] = jnp.sum(grad_n1, axis=0, keepdims=True)

    for j in range(32):
        for t in range(6):
            part = slice(t * 128, t * 128 + 128)
            put(late, 3, j, t, jnp.where(last_row, row_s[0:1, part], qp_s[8 * j : 8 * j + 8, part]))
    pair_late = send(late.at[1 - core], pair_l, pl_ss, pl_rs, twin)

    grad_x = grad_a + norm_back(grad_n1, gain1, unit1, inv1)

    def put_dxa(w, block):
        dxa[:, w] = block

    put_tokens(put_dxa, grad_x)
    home = []
    for slot, (hh, wh) in enumerate(((1, 0), (0, 0), (1, 1))):
        home.append(
            send(
                dxa.at[pl.ds(hh * 6, 6), pl.ds(wh * 3, 3)],
                back.at[pl.ds(6 - hh * 6, 6), pl.ds(3 - wh * 3, 3)],
                back_ss.at[slot], back_rs.at[slot], at(hh, wh - 1),
            )
        )
    back[6:12, 0:3] = dxa[0:6, 3:6]

    diff = halves(jnp.concatenate([diff_s[l] for l in range(3)], axis=1))
    lanes_back = one(diff[0], order[...], 1, 1) + one(diff[1], order[...], 1, 1)
    tail = one(diff[0], rest[...], 1, 0) + one(diff[1], rest[...], 1, 0)
    row_id = lax.broadcasted_iota(jnp.int32, tail.shape, 0) & 7
    lane_id = lax.broadcasted_iota(jnp.int32, tail.shape, 1) // 8
    tail = jnp.where(row_id == lane_id, tail, 0.0).reshape(ZH, 8, 128).sum(axis=1)
    for l in range(2):
        tab_s[l] = lanes_back[:, l * 128 : l * 128 + 128]
    tab_s[0, pl.ds(6, ZH, stride=8), :] = tail
    for k in range(8):
        for l in range(2):
            tabs[2 * k + l] = tab_s[l, 24 * k : 24 * k + 24, :]

    tab_copies = []
    for d in range(1, 16):
        to = lax.rem(plane + d, 16)
        tab_copies.append(send(tabs.at[to], tab_rx.at[d - 1], t_ss.at[d - 1], t_rs.at[d - 1], (lat, zh * 16 + to)))

    pair_late.wait_recv()
    add_pair(late, pair_l)
    first_late = send_first(pair_l, a_l, al_ss, al_rs)
    for copy in first_early:
        copy.wait_recv()
    add_first(pair_e, a_e, acc_ae)
    second_early = send_second(acc_ae, b_e, be_ss, be_rs)

    for copy in first_late:
        copy.wait_recv()
    add_first(pair_l, a_l, acc_al)
    second_late = send_second(acc_al, b_l, bl_ss, bl_rs)

    for copy in second_early:
        copy.wait_recv()
    acc_b[:, 3:8] = (acc_ae[second] + b_e[0]) + (b_e[1] + b_e[2])
    for copy in second_late:
        copy.wait_recv()
    acc_b[:, 0:3] = (acc_al[second] + b_l[0]) + (b_l[1] + b_l[2])
    z_copies = []
    for d in (8, 7, 9, 6, 10, 5, 11, 4, 12, 3, 13, 2, 14, 1, 15):
        to = lax.rem(zh * 8 + zl + d, 16)
        z_copies.append(
            send(
                acc_b.at[to // 8, lax.rem(to, 8)], z_in.at[d - 1], z_ss.at[d - 1], z_rs.at[d - 1],
                (lax.rem(to, 8) * 2 + core, (to // 8) * 16 + plane),
            )
        )

    for copy in tab_copies:
        copy.wait_recv()
    total = tabs[plane]
    for d in range(15):
        total = total + tab_rx[d]
    tab_sum[...] = total
    tab_across = send(tab_sum, tab_pair, tp_ss, tp_rs, (lat, lax.rem(lon + 16, 32)))

    tab_across.wait_recv()
    tab_all[plane] = tab_sum[...] + tab_pair[...]
    tab_back = []
    for d in range(1, 16):
        to = lax.rem(plane + d, 16)
        tab_back.append(
            send(tab_all.at[plane], tab_all.at[plane], tg_ss.at[d - 1], tg_rs.at[d - 1], (lat, zh * 16 + to))
        )

    for copy in z_copies:
        copy.wait_recv()
    total = acc_b[zh, zl]
    for d in range(15):
        total = total + z_in[d]
    slot = core * 8 + zl
    mine[...] = total
    gather[slot] = total
    g_copies = []
    for d in range(1, 16):
        to = lax.rem(lat + d, 16)
        g_copies.append(send(mine, gather.at[slot], g_ss.at[d - 1], g_rs.at[d - 1], (to, lon)))

    for copy in tab_back:
        copy.wait_recv()
    for k in range(8):
        for l in range(2):
            wide_s[l, 24 * k : 24 * k + 24, :] = tab_all[2 * k + l]
    tail = wide_s[0, pl.ds(6, ZH, stride=8), :]
    for h in range(HEADS):
        moved = tail if h == 0 else pltpu.roll(tail, 128 - 8 * h, axis=1)
        wide_s[2, pl.ds(h, ZH, stride=8), :] = moved
    for zn in range(2):
        for hn in range(12):
            spot = hn * 2 + 1 - zn
            block = jnp.concatenate([wide_s[l, spot * 8 : spot * 8 + 8, :] for l in range(3)], axis=1)
            for zm in range(2):
                start = ((zn * 2 + zm) * 12 + hn) * FLAT
                for h in range(HEADS):
                    table_o[h, :, start : start + FLAT] = block[h : h + 1, zm * FLAT : (zm + 1) * FLAT]

    for copy in home:
        copy.wait_recv()
    for copy in g_copies:
        copy.wait_recv()
    for copy in every:
        copy.wait_send()


def kernel_b(
    keep, gather, table_i, back, other,
    fields_grad, n1g_o, n1s_o, qkvw_o, qkvb_o, table_o, projw_o, projb_o, n2g_o, n2s_o, inw_o, inb_o, outw_o,
):
    table_o[...] = table_i[...]
    first_kept = keep[0, 0] == 1
    fields_grad[0] = jnp.where(first_kept, back[...], other[...])
    fields_grad[1] = jnp.where(first_kept, other[...], back[...])

    def late(t):
        return gather.at[(t // 3) * 8 + t % 3]

    def early(t):
        return gather.at[(t // 5) * 8 + 3 + t % 5]

    def strip(tile, row, rows):
        return jnp.concatenate([tile(t)[row : row + rows, :] for t in range(6)], axis=1)

    sums = strip(late, 0, 6)
    qkvw_o[...] = sums[:, 0 : 3 * C]
    projw_o[...] = sums[:, 3 * C : 4 * C]
    inw_o[...] = strip(early, 0, 6)
    small = strip(late, 6, 1)
    qkvb_o[...] = small[:, 0 : 3 * C].reshape(3 * C)
    projb_o[...] = small[:, 3 * C : 4 * C].reshape(C)
    inb_o[...] = strip(early, 6, 1).reshape(HID)
    norms = strip(late, 7, 1)
    for i, ref in enumerate((n1g_o, n1s_o, n2g_o, n2s_o)):
        ref[...] = norms[:, i * C : (i + 1) * C].reshape(C)
    for k in range(3):
        outw_o[8 * k : 8 * k + 8, 0:128] = early(6 + k)[...]
    mix = early(9)[...]
    outw_o[0:8, 128:192] = mix[:, 0:64]
    outw_o[8:16, 128:192] = pltpu.roll(mix, 64, axis=1)[:, 0:64]
    for k in range(4):
        line = early(k)[7:8, :]
        outw_o[16 + 2 * k : 17 + 2 * k, 128:192] = line[:, 0:64]
        outw_o[17 + 2 * k : 18 + 2 * k, 128:192] = pltpu.roll(line, 64, axis=1)[:, 0:64]


def shape(*dims):
    return jax.ShapeDtypeStruct(dims, f32)


def vmem():
    return pl.BlockSpec(memory_space=pltpu.VMEM)


def smem():
    return pl.BlockSpec(memory_space=pltpu.SMEM)


def per_device(lats, lons, fields, cotangent, keep_mask, region_ids, *weights):
    order, rest = (jnp.asarray(m, bf16) for m in bias_order())
    spread = jnp.asarray(spread_order(), bf16)
    weights = list(weights)
    weights[4] = weights[4].transpose(1, 0, 2)
    weights[-1] = weights[-1].T
    grid_order = (0, 2, 3, 1, 4)
    one_sem = pltpu.SemaphoreType.DMA

    def sems(count):
        return pltpu.SemaphoreType.DMA((count,))

    def buf(*dims):
        return pltpu.VMEM(dims, f32)

    arrays = (
        fields.transpose(grid_order), cotangent.transpose(grid_order), region_ids.transpose(2, 0, 1),
        *weights, order, rest, spread,
    )
    tile = (8, 128)
    block = (12, 6, 2, C)
    packed = pl.pallas_call(
        functools.partial(kernel_a, lats, lons),
        out_shape=(shape(16, 8, 128), shape(*(HEADS, 1, 6336)), shape(*block), shape(*block)),
        in_specs=[smem()] + [pl.BlockSpec(memory_space=pl.ANY)] * 18,
        out_specs=(vmem(),) * 4,
        scratch_shapes=[
            *[pltpu.VMEM(a.shape, a.dtype) for a in arrays], sems(18),
            buf(*block), buf(*block), buf(*block), buf(*block), buf(*block), pltpu.VMEM((6, 2, 12), jnp.int32),
            buf(2, 4, 4, 2, 5, *tile), buf(2, 4, 4, 2, 3, *tile),
            buf(4, 4, 2, 5, *tile), buf(4, 4, 2, 3, *tile),
            buf(3, 4, 2, 5, *tile), buf(3, 4, 2, 3, *tile),
            buf(3, 2, 5, *tile), buf(3, 2, 3, *tile),
            buf(4, 2, 5, *tile), buf(4, 2, 3, *tile),
            buf(2, 8, *tile), buf(15, *tile), buf(*tile),
            buf(16, 24, 128), buf(15, 24, 128), buf(24, 128), buf(24, 128), buf(16, 24, 128), buf(3, 192, 128),
            buf(192, 384), buf(3, 192, 128), buf(HEADS, TOK, TOK), buf(3, 192, 128),
            buf(256, 768), buf(8, 768), buf(2, 192, 128),
            sems(3), sems(3), sems(3), sems(3), one_sem, one_sem, sems(3), sems(3),
            one_sem, one_sem, one_sem, one_sem,
            sems(3), sems(3), sems(3), sems(3), sems(3), sems(3), sems(3), sems(3),
            sems(15), sems(15), sems(15), sems(15), sems(15), sems(15), one_sem, one_sem, sems(15), sems(15),
        ],
        compiler_params=pltpu.CompilerParams(collective_id=0, has_side_effects=True, vmem_limit_bytes=VMEM_LIMIT),
        name="block_both_ways",
    )(keep_mask, *arrays)
    outs = list(
        pl.pallas_call(
            kernel_b,
            out_shape=(
                shape(2, *block), shape(C), shape(C), shape(6, 3 * C), shape(3 * C), shape(*(HEADS, 1, 6336)),
                shape(6, C), shape(C), shape(C), shape(C), shape(6, HID), shape(HID), shape(24, C),
            ),
            in_specs=[smem()] + [vmem()] * 4,
            out_specs=(vmem(),) * 13,
            compiler_params=pltpu.CompilerParams(vmem_limit_bytes=VMEM_LIMIT),
            name="unpack",
        )(keep_mask, *packed)
    )
    outs[0] = outs[0].transpose(0, 3, 1, 2, 4)
    outs[5] = outs[5].transpose(1, 0, 2)
    return tuple(outs)


def solution(mesh):
    grid = P(None, None, "lat", "lon", None)
    rows = P("lon", None)
    return jax.shard_map(
        functools.partial(per_device, mesh.shape["lat"], mesh.shape["lon"]),
        mesh=mesh,
        in_specs=(grid, grid, P(), P(None, "lat", "lon"), P(), P(), P(), P(), P("lat", None, None))
        + (P(),) * 7,
        out_specs=(grid, P(), P(), rows, P(), P("lat", None, None), rows, P(), P(), P(), rows, P(), rows),
        check_vma=False,
    )
```

```python
import functools
import math

import jax
import jax.numpy as jnp
import numpy as np
from jax import lax
from jax.experimental import pallas as pl
from jax.experimental.pallas import tpu as pltpu
from jax.sharding import PartitionSpec as P

f32 = jnp.float32
bf16 = jnp.bfloat16
MESH = pl.DeviceIdType.MESH
C = 192
HEADS = 6
HID = 768
TOK = 144
ZH = 24
REL = 11
FLAT = 132
eps = 1e-05
kept = 1.25
scale = 1.0 / math.sqrt(32.0)
VMEM_LIMIT = 56 * 1024 * 1024


def bias_order():
    to = np.zeros((384, 384), np.float32)
    rest = np.zeros((384, 128), np.float32)
    for z in range(2):
        for h in range(12):
            for r in range(REL):
                lane = z * FLAT + h * REL + r
                spot = (REL - 1 - r) * ZH + h * 2 + 1 - z
                to[lane, spot] = 1.0
                if lane >= 256:
                    for head in range(HEADS):
                        rest[spot, 8 * head + lane - 256] = 1.0
    return to, rest


def spread_order():
    to = np.zeros((C, 256), np.float32)
    for feature in range(C):
        to[feature, 8 * (feature // 6) + feature % 6] = 1.0
    return to


def halves(values):
    high = values.astype(bf16)
    return high, (values - high.astype(f32)).astype(bf16)


def thirds(values):
    high = values.astype(bf16)
    left = values - high.astype(f32)
    mid = left.astype(bf16)
    return high, mid, (left - mid.astype(f32)).astype(bf16)


def one(a, b, ca, cb):
    return lax.dot_general(a, b, (((ca,), (cb,)), ((), ())), preferred_element_type=f32)


def product(a, b, cb=0):
    rows = a[0].shape[0]
    first = one(jnp.concatenate(a, axis=0), b[0], 1, cb)
    return first[:rows] + (first[rows:] + one(a[0], b[1], 1, cb))


def outer(a, b):
    return one(a[0], b[0], 0, 0) + (one(a[0], b[1], 0, 0) + one(a[1], b[0], 0, 0))


def norm_parts(values):
    center = values - jnp.mean(values, axis=-1, keepdims=True)
    spread = jnp.mean(center * center, axis=-1, keepdims=True)
    inv = lax.rsqrt(spread + eps)
    return center * inv, inv


def norm_back(grad, gain, unit, inv):
    scaled = grad * gain
    return inv * (
        scaled
        - jnp.mean(scaled, axis=-1, keepdims=True)
        - unit * jnp.mean(scaled * unit, axis=-1, keepdims=True)
    )


def neighbour(lat, lon, lats, lons, dlat, dlon):
    return lax.rem(lat + dlat + lats, lats), lax.rem(lon + dlon + lons, lons)


def take_tokens(read):
    return jnp.concatenate([read(w).reshape(ZH, C) for w in range(6)], axis=0)


def put_tokens(write, values):
    for w in range(6):
        write(w, values[w * ZH : (w + 1) * ZH, :].reshape(12, 2, C))


def kernel_a(
    lats, lons,
    keep, *refs,
):
    hbm, refs = refs[0:18], refs[18:]
    results, refs = refs[0:4], refs[4:]
    loaded, refs = refs[0:18], refs[18:]
    compute_and_sum(lats, lons, keep, hbm, loaded, *results, *loaded, *refs)


def compute_and_sum(
    lats, lons, keep, hbm, loaded,
    gather, table_o, back, other,
    fields, cotg, region, n1g, n1s, wqkv, bqkv, table, wproj, bproj, n2g, n2s, win_w, b_in, wout,
    order, rest, spread,
    load_sem, sel_x, sel_c, win_x, win_c, dxa, region_win,
    early, late, pair_e, pair_l, a_e, a_l, b_e, b_l, acc_ae, acc_al, acc_b, z_in, mine,
    tabs, tab_rx, tab_pair, tab_sum, tab_all, wide_s,
    tab_in, bias_s, attn_s, attn_hi, attn_lo, score_hi, score_lo, diff_s, qp_s, row_s, tab_s,
    hx_ss, hx_rs, hc_ss, hc_rs, reg_ss, reg_rs, back_ss, back_rs, pe_ss, pe_rs, pl_ss, pl_rs, ae_ss, ae_rs, al_ss, al_rs,
    be_ss, be_rs, bl_ss, bl_rs, z_ss, z_rs, g_ss, g_rs, t_ss, t_rs, tp_ss, tp_rs, tg_ss, tg_rs,
):
    lat = lax.axis_index("lat")
    lon = lax.axis_index("lon")
    core = lax.rem(lat, 2)
    zl = lat // 2
    zh = lon // 16
    plane = lax.rem(lon, 16)
    px = plane // 4
    py = lax.rem(plane, 4)
    at = functools.partial(neighbour, lat, lon, lats, lons)
    every = []

    def send(src, dst, ss, rs, device):
        copy = pltpu.make_async_remote_copy(
            src_ref=src, dst_ref=dst, send_sem=ss, recv_sem=rs, device_id=device, device_id_type=MESH
        )
        copy.start()
        every.append(copy)
        return copy

    barrier = pltpu.get_barrier_semaphore()

    def hello(device):
        pl.semaphore_signal(barrier, inc=1, device_id=device, device_id_type=MESH)

    hello(at(1, -1))
    hello(at(0, -1))
    hello(at(-1, 1))
    hello(at(0, 1))
    hello(at(1, 0))
    hello(at(-1, 0))
    for d in range(0, 16, 2):
        hello((lax.rem(lat + d, 16), lax.rem(lon + 16, 32)))
    for d in range(1, 16):
        hello((lax.rem(lat + d, 16), lon))
        hello((lat, zh * 16 + lax.rem(plane + d, 16)))

    loads = [pltpu.make_async_copy(hbm[i], loaded[i], load_sem.at[i]) for i in range(18)]
    for i in (0, 1, 7, 15, 2, 5, 8, 12, 14, 16, 17, 3, 4, 6, 9, 10, 11, 13):
        loads[i].start()
    attn_sample = 1 - keep[0, 0]
    loads[0].wait()
    loads[1].wait()
    sel_x[...] = fields[attn_sample]
    sel_c[...] = cotg[attn_sample]
    win_x[0:6, 3:6] = sel_x[6:12, 0:3]
    win_c[0:6, 3:6] = sel_c[6:12, 0:3]

    halo_x = []
    halo_c = []
    quadrants = ((0, 1), (1, 1), (0, 0))

    def start_halo(src, dst, ss, rs, copies):
        for slot, (sh, sw) in enumerate(quadrants):
            copies.append(
                send(
                    src.at[pl.ds(sh * 6, 6), pl.ds(sw * 3, 3)],
                    dst.at[pl.ds(6 - sh * 6, 6), pl.ds(3 - sw * 3, 3)],
                    ss.at[slot], rs.at[slot], at(sh - 1, sw),
                )
            )

    pl.semaphore_wait(barrier, 6 + 30 + 8)
    start_halo(sel_x, win_x, hx_ss, hx_rs, halo_x)
    loads[2].wait()
    regions = send(region, region_win, reg_ss, reg_rs, at(0, 1))

    for i in (7, 15):
        loads[i].wait()

    tab_in[...] = jnp.zeros(tab_in.shape, f32)
    for zn in range(2):
        for hn in range(12):
            spot = hn * 2 + 1 - zn
            for zm in range(2):
                start = ((zn * 2 + zm) * 12 + hn) * FLAT
                tab_in[spot * 8 : spot * 8 + HEADS, zm * FLAT : (zm + 1) * FLAT] = jnp.concatenate(
                    [table[h, :, start : start + FLAT] for h in range(HEADS)], axis=0
                )
    shifted = None
    for part in thirds(tab_in[...]):
        term = one(part, order[...], 1, 0)
        shifted = term if shifted is None else shifted + term
    for l in range(3):
        bias_s[l] = shifted[:, l * 128 : l * 128 + 128]

    for i in (5, 8, 12, 14, 16, 17, 3, 4, 6, 9, 10, 11, 13):
        loads[i].wait()
    w_qkv = halves(wqkv[...])
    w_proj = halves(wproj[...])
    w_in = halves(win_w[...])
    w_out = halves(wout[...])

    loc_x = take_tokens(lambda w: fields[1 - attn_sample, :, w])
    loc_cot = take_tokens(lambda w: cotg[1 - attn_sample, :, w])
    start_halo(sel_c, win_c, hc_ss, hc_rs, halo_c)

    regions.wait_recv()
    marks = jnp.concatenate([region_win[w] for w in range(6)], axis=0).astype(bf16)
    pick = lax.broadcasted_iota(jnp.int32, (ZH, 12), 0) // 2 == lax.broadcasted_iota(jnp.int32, (ZH, 12), 1)
    marks = one(pick.astype(bf16), marks, 1, 1)
    lane12 = lax.broadcasted_iota(jnp.int32, (ZH, 12), 1)
    level = 1 - (lax.broadcasted_iota(jnp.int32, (ZH, 12), 0) & 1)
    columns = []
    for w in range(6):
        column = jnp.sum(jnp.where(lane12 == 2 * w + level, marks, 0.0), axis=1, keepdims=True)
        columns.append(jnp.broadcast_to(column, (ZH, TOK)))
    mark_rows = jnp.concatenate(columns, axis=0)
    same = mark_rows == mark_rows.T

    for copy in halo_x:
        copy.wait_recv()

    x = take_tokens(lambda w: win_x[:, w])
    unit1, inv1 = norm_parts(x)
    gain1 = n1g[...].reshape(1, C)
    normed1 = halves(unit1 * gain1 + n1s[...].reshape(1, C))
    proj = product(normed1, w_qkv) + bqkv[...].reshape(1, 3 * C)
    query_f = proj[:, 0:C] * scale
    query = halves(query_f)
    key = halves(proj[:, C : 2 * C])
    value = halves(proj[:, 2 * C : 3 * C])
    lanes = lax.broadcasted_iota(jnp.int32, (1, C), 1)
    masks = [(lanes // 32 == h) for h in range(HEADS)]

    def by_head(pair):
        zero = jnp.zeros((), bf16)
        return tuple(jnp.concatenate([jnp.where(mask, part, zero) for mask in masks], axis=0) for part in pair)

    def of_head(values, h):
        return values[h * TOK : (h + 1) * TOK]

    def own_lanes(values):
        result = of_head(values, 0)
        for h in range(1, HEADS):
            result = jnp.where(masks[h], of_head(values, h), result)
        return result

    all_scores = product(by_head(query), key, 1)
    for h in range(HEADS):
        strip = jnp.concatenate([bias_s[l, pl.ds(h, ZH, stride=8), :] for l in range(3)], axis=1)
        bias = jnp.concatenate(
            [pltpu.roll(strip, (384 - (5 - wn) * ZH) % 384, axis=1)[:, 0:TOK] for wn in range(6)], axis=0
        )
        scores = jnp.where(same, of_head(all_scores, h) + bias, -1e30)
        scores = jnp.exp(scores - jnp.max(scores, axis=-1, keepdims=True))
        attn = scores / jnp.sum(scores, axis=-1, keepdims=True)
        attn_s[h] = attn
        attn_hi[h * TOK : (h + 1) * TOK, :], attn_lo[h * TOK : (h + 1) * TOK, :] = halves(attn)
    mixed = own_lanes(product((attn_hi[...], attn_lo[...]), value))
    mixed = halves(mixed)
    branch = product(mixed, w_proj) + bproj[...].reshape(1, C)

    for copy in halo_c:
        copy.wait_recv()
    cot = take_tokens(lambda w: win_c[:, w])
    both = keep[0, 0] == keep[0, 1]
    middle = jnp.where(both, x + kept * branch, loc_x)
    cot_m = jnp.where(both, cot, loc_cot)
    unit2, inv2 = norm_parts(middle)
    gain2 = n2g[...].reshape(1, C)
    normed2 = halves(unit2 * gain2 + n2s[...].reshape(1, C))
    hidden = product(normed2, w_in) + b_in[...].reshape(1, HID)
    cdf = 0.5 * (1.0 + lax.erf(hidden * math.sqrt(0.5)))
    slope = cdf + hidden * jnp.exp(-0.5 * hidden * hidden) * (1.0 / math.sqrt(2.0 * math.pi))
    grad_y = halves(kept * cot_m)
    grad_hidden = halves(product(grad_y, w_out) * slope)
    grad_out_w = outer(halves(hidden * cdf), grad_y)

    ones_lane = (lax.broadcasted_iota(jnp.int32, (1, 256), 1) & 7) == 6

    def spread_out(pair):
        high = one(pair[0], spread[...], 1, 0)
        low = one(pair[1], spread[...], 1, 0)
        return jnp.where(ones_lane, 1.0, high).astype(bf16), low.astype(bf16)

    grad_in_w = outer(spread_out(normed2), grad_hidden)

    low_lanes = lax.broadcasted_iota(jnp.int32, (8, 128), 1) < 64

    def put(buffer, count, j, tile_id, tile, rows=slice(None)):
        zh_j, a, b = j // 16, j // 4 % 4, j % 4
        if tile_id < count:
            buffer[0, a, b, zh_j, tile_id, rows, :] = tile
        else:
            buffer[1, b, a, zh_j, tile_id - count, rows, :] = tile

    last_row = lax.broadcasted_iota(jnp.int32, (8, 128), 0) == 7
    for j in range(32):
        block = grad_out_w[24 * j : 24 * j + 24, :]
        tails = [
            jnp.concatenate([block[8 * k : 8 * k + 8, 128:192], jnp.zeros((8, 64), f32)], axis=1) for k in range(3)
        ]
        for k in range(3):
            put(early, 5, j, 6 + k, block[8 * k : 8 * k + 8, 0:128])
        put(early, 5, j, 9, tails[0] + pltpu.roll(tails[1], 64, axis=1))
        pairs = tails[2] + pltpu.roll(pltpu.roll(tails[2], 64, axis=1), 7, axis=0)
        for t in range(6):
            tile = grad_in_w[8 * j : 8 * j + 8, t * 128 : t * 128 + 128]
            if t < 4:
                tile = jnp.where(last_row, pairs[2 * t : 2 * t + 1, :], tile)
            put(early, 5, j, t, tile)
    twin = (lat + 1 - 2 * core, lon)
    pair_early = send(early.at[1 - core], pair_e, pe_ss, pe_rs, twin)

    grad_n2 = product(grad_hidden, w_in, 1)
    row_s[0:1, 2 * C : 3 * C] = jnp.sum(grad_n2 * unit2, axis=0, keepdims=True)
    row_s[0:1, 3 * C : 4 * C] = jnp.sum(grad_n2, axis=0, keepdims=True)
    grad_m = cot_m + norm_back(grad_n2, gain2, unit2, inv2)
    grad_a = jnp.where(both, grad_m, cot)

    def put_other(w, block):
        other[:, w] = block

    put_tokens(put_other, jnp.where(both, loc_cot, grad_m))

    first = px + core * (py - px)
    second = py + core * (px - py)

    def along(pos_first, pos_second):
        x_pos = pos_first + core * (pos_second - pos_first)
        y_pos = pos_second + core * (pos_first - pos_second)
        return lat, zh * 16 + x_pos * 4 + y_pos

    def add_pair(buffer, arrived):
        for i in range(4):
            for j in range(4):
                arrived[i, j] = arrived[i, j] + buffer[core, i, j]

    def send_first(arrived, slots, ss, rs):
        copies = []
        for d in range(1, 4):
            to = lax.rem(first + d, 4)
            copies.append(send(arrived.at[to], slots.at[d - 1], ss.at[d - 1], rs.at[d - 1], along(to, second)))
        return copies

    def add_first(arrived, slots, acc):
        for j in range(4):
            acc[j] = (arrived[first, j] + slots[0, j]) + (slots[1, j] + slots[2, j])

    def send_second(acc, slots, ss, rs):
        copies = []
        for d in range(1, 4):
            to = lax.rem(second + d, 4)
            copies.append(send(acc.at[to], slots.at[d - 1], ss.at[d - 1], rs.at[d - 1], along(first, to)))
        return copies

    grad_b = halves(kept * grad_a)
    qp_s[:, 3 * C : 4 * C] = outer(spread_out(mixed), grad_b)
    grad_o = product(grad_b, w_proj, 1)
    grad_o_t = halves(grad_o.T)
    query_t = halves(query_f.T)
    all_grad = product(by_head(halves(grad_o)), value, 1)
    diff_s[...] = jnp.zeros(diff_s.shape, f32)
    first_early = None
    grad_v = []
    grad_k = []
    for h in range(HEADS):
        attn = attn_s[h]
        term = attn * of_head(all_grad, h)
        grad_s = term - attn * jnp.sum(term, axis=-1, keepdims=True)
        grad_sp = halves(grad_s)
        rows = slice(h * TOK, (h + 1) * TOK)
        score_hi[rows, :], score_lo[rows, :] = grad_sp
        head = slice(h * 32, h * 32 + 32)
        grad_v.append(product(tuple(part[head, :] for part in grad_o_t), (attn_hi[rows, :], attn_lo[rows, :])))
        grad_k.append(product(tuple(part[head, :] for part in query_t), grad_sp))
        wide = jnp.concatenate([grad_s, jnp.zeros((TOK, 384 - TOK), f32)], axis=1)
        total = None
        for wn in range(6):
            block = wide[wn * ZH : (wn + 1) * ZH, :]
            if wn < 5:
                block = pltpu.roll(block, (5 - wn) * ZH, axis=1)
            total = block if total is None else total + block
        for l in range(3):
            diff_s[l, pl.ds(h, ZH, stride=8), :] = total[:, l * 128 : l * 128 + 128]
        if h == 1:
            pair_early.wait_recv()
            add_pair(early, pair_e)
            first_early = send_first(pair_e, a_e, ae_ss, ae_rs)
    grad_q = own_lanes(product((score_hi[...], score_lo[...]), key))
    grad_k = jnp.concatenate(grad_k, axis=0).T
    grad_v = jnp.concatenate(grad_v, axis=0).T
    grad_p = halves(jnp.concatenate([grad_q * scale, grad_k, grad_v], axis=1))
    qp_s[:, 0 : 3 * C] = outer(spread_out(normed1), grad_p)
    grad_n1 = product(grad_p, w_qkv, 1)
    row_s[0:1, 0:C] = jnp.sum(grad_n1 * unit1, axis=0, keepdims=True)
    row_s[0:1, C : 2 * C] = jnp.sum(grad_n1, axis=0, keepdims=True)

    for j in range(32):
        for t in range(6):
            part = slice(t * 128, t * 128 + 128)
            put(late, 3, j, t, jnp.where(last_row, row_s[0:1, part], qp_s[8 * j : 8 * j + 8, part]))
    pair_late = send(late.at[1 - core], pair_l, pl_ss, pl_rs, twin)

    grad_x = grad_a + norm_back(grad_n1, gain1, unit1, inv1)

    def put_dxa(w, block):
        dxa[:, w] = block

    put_tokens(put_dxa, grad_x)
    home = []
    for slot, (hh, wh) in enumerate(((1, 0), (0, 0), (1, 1))):
        home.append(
            send(
                dxa.at[pl.ds(hh * 6, 6), pl.ds(wh * 3, 3)],
                back.at[pl.ds(6 - hh * 6, 6), pl.ds(3 - wh * 3, 3)],
                back_ss.at[slot], back_rs.at[slot], at(hh, wh - 1),
            )
        )
    back[6:12, 0:3] = dxa[0:6, 3:6]

    diff = halves(jnp.concatenate([diff_s[l] for l in range(3)], axis=1))
    lanes_back = one(diff[0], order[...], 1, 1) + one(diff[1], order[...], 1, 1)
    tail = one(diff[0], rest[...], 1, 0) + one(diff[1], rest[...], 1, 0)
    row_id = lax.broadcasted_iota(jnp.int32, tail.shape, 0) & 7
    lane_id = lax.broadcasted_iota(jnp.int32, tail.shape, 1) // 8
    tail = jnp.where(row_id == lane_id, tail, 0.0).reshape(ZH, 8, 128).sum(axis=1)
    for l in range(2):
        tab_s[l] = lanes_back[:, l * 128 : l * 128 + 128]
    tab_s[0, pl.ds(6, ZH, stride=8), :] = tail
    for k in range(8):
        for l in range(2):
            tabs[2 * k + l] = tab_s[l, 24 * k : 24 * k + 24, :]

    tab_copies = []
    for d in range(1, 16):
        to = lax.rem(plane + d, 16)
        tab_copies.append(send(tabs.at[to], tab_rx.at[d - 1], t_ss.at[d - 1], t_rs.at[d - 1], (lat, zh * 16 + to)))

    pair_late.wait_recv()
    add_pair(late, pair_l)
    first_late = send_first(pair_l, a_l, al_ss, al_rs)
    for copy in first_early:
        copy.wait_recv()
    add_first(pair_e, a_e, acc_ae)
    second_early = send_second(acc_ae, b_e, be_ss, be_rs)

    for copy in first_late:
        copy.wait_recv()
    add_first(pair_l, a_l, acc_al)
    second_late = send_second(acc_al, b_l, bl_ss, bl_rs)

    for copy in second_early:
        copy.wait_recv()
    acc_b[:, 3:8] = (acc_ae[second] + b_e[0]) + (b_e[1] + b_e[2])
    for copy in second_late:
        copy.wait_recv()
    acc_b[:, 0:3] = (acc_al[second] + b_l[0]) + (b_l[1] + b_l[2])
    z_copies = []
    for d in (8, 7, 9, 6, 10, 5, 11, 4, 12, 3, 13, 2, 14, 1, 15):
        to = lax.rem(zh * 8 + zl + d, 16)
        z_copies.append(
            send(
                acc_b.at[to // 8, lax.rem(to, 8)], z_in.at[d - 1], z_ss.at[d - 1], z_rs.at[d - 1],
                (lax.rem(to, 8) * 2 + core, (to // 8) * 16 + plane),
            )
        )

    for copy in tab_copies:
        copy.wait_recv()
    total = tabs[plane]
    for d in range(15):
        total = total + tab_rx[d]
    tab_sum[...] = total
    tab_across = send(tab_sum, tab_pair, tp_ss, tp_rs, (lat, lax.rem(lon + 16, 32)))

    tab_across.wait_recv()
    tab_all[plane] = tab_sum[...] + tab_pair[...]
    tab_back = []
    for d in range(1, 16):
        to = lax.rem(plane + d, 16)
        tab_back.append(
            send(tab_all.at[plane], tab_all.at[plane], tg_ss.at[d - 1], tg_rs.at[d - 1], (lat, zh * 16 + to))
        )

    for copy in z_copies:
        copy.wait_recv()
    total = acc_b[zh, zl]
    for d in range(15):
        total = total + z_in[d]
    slot = core * 8 + zl
    mine[...] = total
    gather[slot] = total
    g_copies = []
    for d in range(1, 16):
        g_copies.append(
            pltpu.make_async_remote_copy(
                src_ref=mine, dst_ref=gather.at[slot], send_sem=g_ss.at[d - 1], recv_sem=g_rs.at[d - 1],
                device_id=(lax.rem(lat + d, 16), lon), device_id_type=MESH,
            )
        )
    every.extend(g_copies)

    @pl.when(zl < 4)
    def _():
        for copy in reversed(g_copies):
            copy.start()

    @pl.when(zl >= 4)
    def _():
        for copy in g_copies:
            copy.start()


    for copy in tab_back:
        copy.wait_recv()
    for k in range(8):
        for l in range(2):
            wide_s[l, 24 * k : 24 * k + 24, :] = tab_all[2 * k + l]
    tail = wide_s[0, pl.ds(6, ZH, stride=8), :]
    for h in range(HEADS):
        moved = tail if h == 0 else pltpu.roll(tail, 128 - 8 * h, axis=1)
        wide_s[2, pl.ds(h, ZH, stride=8), :] = moved
    for zn in range(2):
        for hn in range(12):
            spot = hn * 2 + 1 - zn
            block = jnp.concatenate([wide_s[l, spot * 8 : spot * 8 + 8, :] for l in range(3)], axis=1)
            for zm in range(2):
                start = ((zn * 2 + zm) * 12 + hn) * FLAT
                for h in range(HEADS):
                    table_o[h, :, start : start + FLAT] = block[h : h + 1, zm * FLAT : (zm + 1) * FLAT]

    for copy in home:
        copy.wait_recv()
    for copy in g_copies:
        copy.wait_recv()
    for copy in every:
        copy.wait_send()


def kernel_b(
    keep, gather, table_i, back, other,
    fields_grad, n1g_o, n1s_o, qkvw_o, qkvb_o, table_o, projw_o, projb_o, n2g_o, n2s_o, inw_o, inb_o, outw_o,
):
    table_o[...] = table_i[...]
    first_kept = keep[0, 0] == 1
    fields_grad[0] = jnp.where(first_kept, back[...], other[...])
    fields_grad[1] = jnp.where(first_kept, other[...], back[...])

    def late(t):
        return gather.at[(t // 3) * 8 + t % 3]

    def early(t):
        return gather.at[(t // 5) * 8 + 3 + t % 5]

    def strip(tile, row, rows):
        return jnp.concatenate([tile(t)[row : row + rows, :] for t in range(6)], axis=1)

    sums = strip(late, 0, 6)
    qkvw_o[...] = sums[:, 0 : 3 * C]
    projw_o[...] = sums[:, 3 * C : 4 * C]
    inw_o[...] = strip(early, 0, 6)
    small = strip(late, 6, 1)
    qkvb_o[...] = small[:, 0 : 3 * C].reshape(3 * C)
    projb_o[...] = small[:, 3 * C : 4 * C].reshape(C)
    inb_o[...] = strip(early, 6, 1).reshape(HID)
    norms = strip(late, 7, 1)
    for i, ref in enumerate((n1g_o, n1s_o, n2g_o, n2s_o)):
        ref[...] = norms[:, i * C : (i + 1) * C].reshape(C)
    for k in range(3):
        outw_o[8 * k : 8 * k + 8, 0:128] = early(6 + k)[...]
    mix = early(9)[...]
    outw_o[0:8, 128:192] = mix[:, 0:64]
    outw_o[8:16, 128:192] = pltpu.roll(mix, 64, axis=1)[:, 0:64]
    for k in range(4):
        line = early(k)[7:8, :]
        outw_o[16 + 2 * k : 17 + 2 * k, 128:192] = line[:, 0:64]
        outw_o[17 + 2 * k : 18 + 2 * k, 128:192] = pltpu.roll(line, 64, axis=1)[:, 0:64]


def shape(*dims):
    return jax.ShapeDtypeStruct(dims, f32)


def vmem():
    return pl.BlockSpec(memory_space=pltpu.VMEM)


def smem():
    return pl.BlockSpec(memory_space=pltpu.SMEM)


def per_device(lats, lons, fields, cotangent, keep_mask, region_ids, *weights):
    order, rest = (jnp.asarray(m, bf16) for m in bias_order())
    spread = jnp.asarray(spread_order(), bf16)
    weights = list(weights)
    weights[4] = weights[4].transpose(1, 0, 2)
    weights[-1] = weights[-1].T
    grid_order = (0, 2, 3, 1, 4)
    one_sem = pltpu.SemaphoreType.DMA

    def sems(count):
        return pltpu.SemaphoreType.DMA((count,))

    def buf(*dims):
        return pltpu.VMEM(dims, f32)

    arrays = (
        fields.transpose(grid_order), cotangent.transpose(grid_order), region_ids.transpose(2, 0, 1),
        *weights, order, rest, spread,
    )
    tile = (8, 128)
    block = (12, 6, 2, C)
    packed = pl.pallas_call(
        functools.partial(kernel_a, lats, lons),
        out_shape=(shape(16, 8, 128), shape(*(HEADS, 1, 6336)), shape(*block), shape(*block)),
        in_specs=[smem()] + [pl.BlockSpec(memory_space=pl.ANY)] * 18,
        out_specs=(vmem(),) * 4,
        scratch_shapes=[
            *[pltpu.VMEM(a.shape, a.dtype) for a in arrays], sems(18),
            buf(*block), buf(*block), buf(*block), buf(*block), buf(*block), pltpu.VMEM((6, 2, 12), jnp.int32),
            buf(2, 4, 4, 2, 5, *tile), buf(2, 4, 4, 2, 3, *tile),
            buf(4, 4, 2, 5, *tile), buf(4, 4, 2, 3, *tile),
            buf(3, 4, 2, 5, *tile), buf(3, 4, 2, 3, *tile),
            buf(3, 2, 5, *tile), buf(3, 2, 3, *tile),
            buf(4, 2, 5, *tile), buf(4, 2, 3, *tile),
            buf(2, 8, *tile), buf(15, *tile), buf(*tile),
            buf(16, 24, 128), buf(15, 24, 128), buf(24, 128), buf(24, 128), buf(16, 24, 128), buf(3, 192, 128),
            buf(192, 384), buf(3, 192, 128), buf(HEADS, TOK, TOK),
            *[pltpu.VMEM((HEADS * TOK, TOK), bf16)] * 4, buf(3, 192, 128),
            buf(256, 768), buf(8, 768), buf(2, 192, 128),
            sems(3), sems(3), sems(3), sems(3), one_sem, one_sem, sems(3), sems(3),
            one_sem, one_sem, one_sem, one_sem,
            sems(3), sems(3), sems(3), sems(3), sems(3), sems(3), sems(3), sems(3),
            sems(15), sems(15), sems(15), sems(15), sems(15), sems(15), one_sem, one_sem, sems(15), sems(15),
        ],
        compiler_params=pltpu.CompilerParams(collective_id=0, has_side_effects=True, vmem_limit_bytes=VMEM_LIMIT),
        name="block_both_ways",
    )(keep_mask, *arrays)
    outs = list(
        pl.pallas_call(
            kernel_b,
            out_shape=(
                shape(2, *block), shape(C), shape(C), shape(6, 3 * C), shape(3 * C), shape(*(HEADS, 1, 6336)),
                shape(6, C), shape(C), shape(C), shape(C), shape(6, HID), shape(HID), shape(24, C),
            ),
            in_specs=[smem()] + [vmem()] * 4,
            out_specs=(vmem(),) * 13,
            compiler_params=pltpu.CompilerParams(vmem_limit_bytes=VMEM_LIMIT),
            name="unpack",
        )(keep_mask, *packed)
    )
    outs[0] = outs[0].transpose(0, 3, 1, 2, 4)
    outs[5] = outs[5].transpose(1, 0, 2)
    return tuple(outs)


def solution(mesh):
    grid = P(None, None, "lat", "lon", None)
    rows = P("lon", None)
    return jax.shard_map(
        functools.partial(per_device, mesh.shape["lat"], mesh.shape["lon"]),
        mesh=mesh,
        in_specs=(grid, grid, P(), P(None, "lat", "lon"), P(), P(), P(), P(), P("lat", None, None))
        + (P(),) * 7,
        out_specs=(grid, P(), P(), rows, P(), P("lat", None, None), rows, P(), P(), P(), rows, P(), rows),
        check_vma=False,
    )
```
